512 devices in a mesh: tile: 32 (over y, x), chan: 16 (over z, core).
Axes of the slice: x: 4, y: 8, z: 8, core: 2. Of those that a mesh axis runs over, the one named last changes fastest.
Arguments:
- ensemble: bfloat16 [12288, 128, 256], P('tile', 'chan'), may hold values from -6 to 6
- jacobian: bfloat16 [5120, 512, 128], P('tile', 'chan'), may hold values from -1 to 1
- innovation: float32 [5120, 512], P('tile', 'chan'), may hold values from -6 to 6
- error_vectors: float32 [512, 32], replicated, may hold values from -1 to 1, as said below
- error_values: float32 [512], replicated, may hold values from 0.25 to 4
- ensemble_vectors: float32 [256, 256], replicated, may hold values from -1 to 1, as said below
- column_pick: int32 [32, 5, 40], P('tile'), may hold values from 0 to 383
- footprint_slot: int32 [5120], P('tile'), may hold values from 0 to 199, as said below
- footprint_count: int32 [32], P('tile'), may hold values from 20 to 160, as said below
Outputs:
- analysis: bfloat16 [12288, 128, 256], P('tile', 'chan')
The draws below stay inside these ranges and needn't reach their ends.
Inputs may be any that keep to these rules, and one draw needn't show every extreme that they name: `footprint_slot`: the 160 entries of one pack are distinct; slot o * 40 + j is the j-th column that tile (pack + 2 - o) mod 32 sends to this pack. `footprint_count`: some pack has all 160 footprints live. `error_vectors`: each block of 32 rows is an orthogonal matrix. `ensemble_vectors`: an orthogonal matrix.
All inputs are finite; a program needn't handle non-finite values.
Results may differ from the reference program's by a relative error of at most 0.013.
Values may be sent and summed in bfloat16 or wider, within the bound.
No kernel may reach another device: no remote copies, remote signals or barrier semaphores. Data moves between devices by JAX's collectives and lax.ppermute only.
A program may use at most 64 MiB of HBM per device.

```python
import math
import jax
import jax.numpy as jnp
from jax import lax

ENS = 256
LEV = 128
CH_DEV = 32
REACH = 2
F_DEV = 160
COLS_DEV = 384
SPAN = 5
CAP = 40
CHANNELS = 512
PACKS = 32
FOOTPRINTS = 5120
COLUMNS = 12288


def draw_error_vectors(key, part):
    blocks = jax.random.normal(key, (CHANNELS // CH_DEV, CH_DEV, CH_DEV), jnp.float32)
    basis_blocks = jnp.linalg.qr(blocks)[0]
    return basis_blocks.reshape(CHANNELS, CH_DEV).astype(jnp.float32)


def draw_ensemble_vectors(key, part):
    square = jax.random.normal(key, (ENS, ENS), jnp.float32)
    return jnp.linalg.qr(square)[0].astype(jnp.float32)


def draw_footprint_slot(key, part):
    pack_keys = jax.random.split(jax.random.fold_in(key, 11), PACKS)
    orders = jax.vmap(lambda single: jax.random.permutation(single, SPAN * CAP))(pack_keys)
    return orders[:, :F_DEV].reshape(-1).astype(jnp.int32)


def draw_footprint_count(key, part):
    base_counts = jax.random.randint(jax.random.fold_in(key, 23), (PACKS,), F_DEV // 8, F_DEV // 2 + 1)
    busiest = jax.random.randint(jax.random.fold_in(key, 29), (), 0, PACKS)
    return jnp.where(jnp.arange(PACKS) == busiest, F_DEV, base_counts).astype(jnp.int32)


def smooth_levels(sub_key, leading):
    raw = jax.random.normal(sub_key, leading + (LEV + 15,), jnp.float32)
    summed = jnp.concatenate([jnp.zeros(leading + (1,), jnp.float32), jnp.cumsum(raw, axis=-1)], axis=-1)
    return (summed[..., 16:] - summed[..., :-16]) / 4.0


def draw_jacobian(key, part):
    sigma = (1000.0 / (LEV * FOOTPRINTS * CHANNELS)) ** 0.5
    limit = min(6.0 * sigma, 1.0)
    block_count = FOOTPRINTS // F_DEV

    def one_block(index):
        sub_keys = jax.random.split(jax.random.fold_in(jax.random.fold_in(key, 101), index), 4)
        level_common = jax.random.normal(sub_keys[0], (F_DEV, 1, 1), jnp.float32)
        profile = 0.8 * level_common + 0.6 * smooth_levels(sub_keys[1], (F_DEV, 1))
        channel_part = smooth_levels(sub_keys[2], (F_DEV, CHANNELS))
        white = jax.random.normal(sub_keys[3], (F_DEV, CHANNELS, LEV), jnp.float32)
        values = 0.8 * profile + 0.4 * channel_part + 0.45 * white
        return jnp.clip(values * sigma, -limit, limit)
    blocks = lax.map(one_block, jnp.arange(block_count, dtype=jnp.int32))
    return blocks.reshape(FOOTPRINTS, CHANNELS, LEV).astype(jnp.bfloat16)


def place_ends(array, key, smallest, high):
    dims = array.shape
    spot = [jax.random.randint(jax.random.fold_in(key, axis), (), 0, dims[axis]) for axis in range(len(dims))]
    array = array.at[tuple(spot)].set(smallest)
    longest = dims.index(max(dims))
    spot[longest] = (spot[longest] + 1) % dims[longest]
    return array.at[tuple(spot)].set(high)


def block_levels(stream_key, extent, pieces, least, high):
    factor_of = 1.0
    for dim, parts in pieces:
        draws = jax.random.uniform(jax.random.fold_in(jax.random.fold_in(stream_key, 6), dim), (parts,), jnp.float32, least / len(pieces), high / len(pieces))
        factor_of = factor_of * jnp.repeat(jnp.exp(draws), extent[dim] // parts).reshape((-1,) + (1,) * (len(extent) - 1 - dim))
    return factor_of


def scatter_about(rng, extent, scale, bound, shards=(), kind=jnp.bfloat16):
    array = scale * jax.random.normal(rng, extent, jnp.float32)
    if shards:
        array = array * block_levels(rng, extent, shards, -0.22, 0.18)
    return jnp.clip(array, -bound, bound).astype(kind)


def setup_inputs(seed: int = 0) -> dict:
    splits = jax.random.split(jax.random.key(seed), 10)
    return {
        "ensemble": scatter_about(splits[0], (COLUMNS, LEV, ENS), 1.0, 6.0, ((0, 32), (1, 16))),
        "jacobian": draw_jacobian(jax.random.fold_in(splits[9], 71), 0),
        "innovation": scatter_about(splits[2], (FOOTPRINTS, CHANNELS), 1.0, 6.0, ((0, 32), (1, 16)), jnp.float32),
        "error_vectors": draw_error_vectors(jax.random.fold_in(splits[9], 71), 0),
        "error_values": jnp.clip(jnp.exp(jax.random.uniform(splits[4], (CHANNELS,), jnp.float32, math.log(0.25), math.log(4.0))), 0.25, 4.0),
        "ensemble_vectors": draw_ensemble_vectors(jax.random.fold_in(splits[9], 71), 0),
        "column_pick": place_ends(jax.random.randint(splits[6], (PACKS, SPAN, CAP), 0, COLS_DEV), jax.random.fold_in(splits[6], 1), 0, COLS_DEV - 1).astype(jnp.int32),
        "footprint_slot": draw_footprint_slot(jax.random.fold_in(splits[9], 71), 0),
        "footprint_count": draw_footprint_count(jax.random.fold_in(splits[9], 71), 0),
    }


def turn_blocks(values, vectors):
    row_count, channels, members = values.shape
    group_width = vectors.shape[1]
    grouped = values.reshape(row_count, channels // group_width, group_width, members)
    basis_blocks = vectors.reshape(channels // group_width, group_width, group_width)
    turned = jnp.einsum('gce,fgck->fgek', basis_blocks, grouped, precision=lax.Precision.HIGHEST)
    return turned.reshape(row_count, channels, members)

def turn_rows(values, vectors):
    row_count, channels = values.shape
    group_width = vectors.shape[1]
    grouped = values.reshape(row_count, channels // group_width, group_width)
    basis_blocks = vectors.reshape(channels // group_width, group_width, group_width)
    turned = jnp.einsum('gce,fgc->fge', basis_blocks, grouped, precision=lax.Precision.HIGHEST)
    return turned.reshape(row_count, channels)

def reference(ensemble, jacobian, innovation, error_vectors, error_values, ensemble_vectors, column_pick, footprint_slot, footprint_count):
    members = ensemble.shape[2]
    scales = 1.0 / jnp.sqrt(error_values)

    def pack_terms(carried, pack_index):
        gram_sum, pull_sum = carried
        slot_ids = lax.dynamic_slice_in_dim(footprint_slot, pack_index * F_DEV, F_DEV, 0)
        offset = slot_ids // CAP
        place_ids = slot_ids % CAP
        source = (pack_index + REACH - offset) % PACKS
        local_ids = column_pick[source, offset, place_ids]
        columns = jnp.take(ensemble, (source * COLS_DEV + local_ids).astype(jnp.int32), axis=0)
        sensitivity = lax.dynamic_slice_in_dim(jacobian, pack_index * F_DEV, F_DEV, 0)
        response = jnp.einsum('fcl,flk->fck', sensitivity.astype(jnp.float32), columns.astype(jnp.float32), precision=lax.Precision.HIGHEST)
        live_rows = (jnp.arange(F_DEV, dtype=jnp.int32) < footprint_count[pack_index]).astype(jnp.float32)
        whitened = turn_blocks(response, error_vectors) * scales[None, :, None] * live_rows[:, None, None]
        misfit_rows = lax.dynamic_slice_in_dim(innovation, pack_index * F_DEV, F_DEV, 0)
        misfit = turn_rows(misfit_rows, error_vectors) * scales[None, :]
        pull_sum = pull_sum + jnp.einsum('fck,fc->k', whitened, misfit, precision=lax.Precision.HIGHEST)
        rounded = whitened.astype(jnp.bfloat16).reshape(-1, members)
        gram_sum = gram_sum + lax.dot_general(rounded.astype(jnp.float32), rounded.astype(jnp.float32), (((0,), (0,)), ((), ())), preferred_element_type=jnp.float32)
        return ((gram_sum, pull_sum), None)
    initial = (jnp.zeros((members, members), jnp.float32), jnp.zeros((members,), jnp.float32))
    (gram_sum, pull_sum), _ = lax.scan(pack_terms, initial, jnp.arange(PACKS, dtype=jnp.int32))
    system = gram_sum + (members - 1) * jnp.eye(members, dtype=jnp.float32)
    factor = jnp.linalg.cholesky(system)
    halfway = lax.linalg.triangular_solve(factor, pull_sum[:, None], left_side=True, lower=True)
    mean_weights = lax.linalg.triangular_solve(factor, halfway, left_side=True, lower=True, transpose_a=True)[:, 0]
    spread = jnp.sqrt(members - 1.0) * lax.linalg.triangular_solve(factor, ensemble_vectors, left_side=True, lower=True, transpose_a=True)
    transform = (spread + mean_weights[:, None]).astype(jnp.bfloat16)
    blocks = ensemble.reshape(PACKS, COLS_DEV * LEV, members)

    def update(block):
        return jnp.dot(block.astype(jnp.float32), transform.astype(jnp.float32), preferred_element_type=jnp.float32).astype(jnp.bfloat16)
    return lax.map(update, blocks).reshape(COLUMNS, LEV, members)
```

```python
import jax
import jax.numpy as jnp
from jax import lax
from jax.experimental import pallas as pl
from jax.experimental.pallas import tpu as pltpu
from jax.sharding import Mesh
from jax.sharding import PartitionSpec as P

TILE = ("y", "x")
CHAN = ("z", "c")
NEAR = ("x", "z", "c")
FAR = "y"
MEM = 256
HI = lax.Precision.HIGHEST
F32 = jnp.float32
BF16 = jnp.bfloat16
VM = pl.BlockSpec(memory_space=pltpu.VMEM)
SM = pl.BlockSpec(memory_space=pltpu.SMEM)
PARAMS = pltpu.CompilerParams(vmem_limit_bytes=48 * 2**20)


def cost(flops, size):
    return pl.CostEstimate(flops=flops, bytes_accessed=size, transcendentals=0)


def iota2(rows, columns, dim):
    return lax.broadcasted_iota(jnp.int32, (rows, columns), dim)


def nt(a, b, precision=None):
    return lax.dot_general(
        a, b, (((1,), (1,)), ((), ())), precision=precision, preferred_element_type=F32
    )


def nn(a, b, precision=None):
    return lax.dot_general(
        a, b, (((1,), (0,)), ((), ())), precision=precision, preferred_element_type=F32
    )


def split(x):
    high = x.astype(BF16)
    return high, (x - high.astype(F32)).astype(BF16)


def pick_kernel(pick, ensemble, *sends):
    capacity = sends[0].shape[0]
    for o, out in enumerate(sends):

        def one(j, carry, o=o, out=out):
            out[j] = ensemble[pick[o * capacity + j]]
            return carry

        lax.fori_loop(0, capacity, one, 0, unroll=8)


def weights_kernel(place, innovation, vectors, inverses, jacobian, slabs, sums):
    group = place[0]
    width = vectors.shape[1]
    start = pl.multiple_of(group * width, width)
    basis = vectors[pl.ds(start, width), :]
    scaled = basis * inverses[pl.ds(group, 1), :]
    tiled = nt(scaled, jnp.concatenate([basis] * 8, axis=0), HI)
    weights = nn(innovation[...], tiled, HI)
    mine = iota2(8, 8 * width, 1) // width == iota2(8, 8 * width, 0)
    rows = innovation.shape[0]
    for k in range(rows // 8):
        high, low = split(jnp.where(mine, weights[8 * k : 8 * k + 8], 0.0))
        block = jacobian[8 * k : 8 * k + 8].reshape(8 * width, 128)
        sums[8 * k : 8 * k + 8, :] = nn(high, block) + nn(low, block)
    share = rows // slabs.shape[0]
    zero = jnp.zeros((8 - (share - 8), 128), F32)
    for i in range(slabs.shape[0]):
        left = sums[share * i : share * i + 8, :]
        right = jnp.concatenate([sums[share * i + 8 : share * i + share, :], zero], axis=0)
        slabs[i] = jnp.concatenate([left, right], axis=1).astype(BF16)


def slot_kernel(slot, a0, a1, a2, a3, a4, slabs, out, held):
    capacity = a0.shape[0]
    for o, part in enumerate((a0, a1, a2, a3, a4)):
        held[o * capacity : (o + 1) * capacity] = part[...]
    peers = slabs.shape[0]
    share = out.shape[0] // peers - 1

    def one(i, carry):
        for f in range(share):
            out[i * (share + 1) + f] = held[slot[i * share + f]]
        out[i * (share + 1) + share] = slabs[i]
        return carry

    lax.fori_loop(0, peers, one, 0)


def terms_kernel(place, vectors, scales, jacobian, arrived, out):
    peers = vectors.shape[0] // vectors.shape[1]
    share = jacobian.shape[0] // peers
    first = place[0] * share
    count = place[1]
    half = MEM
    same = iota2(half, half, 0) // 32 == iota2(half, half, 1) // 32
    turns = []
    for h in range(2):
        block = vectors[h * half : (h + 1) * half, :]
        wide = jnp.where(same, jnp.concatenate([block] * 8, axis=1), 0.0) * scales[h : h + 1, :]
        turns.append(split(wide.T))
    b = arrived[share].astype(F32)
    for source in range(1, peers):
        b = b + arrived[source * (share + 1) + share].astype(F32)
    gram = jnp.zeros((MEM, MEM), F32)
    pull = jnp.zeros((8, MEM), F32)
    for f in range(share):
        live = jnp.where(first + f < count, 1.0, 0.0).astype(F32)
        parts = []
        for h in range(2):
            block = jnp.concatenate(
                [jacobian[(h * 8 + s) * share + f] for s in range(8)], axis=0
            )
            high, low = turns[h]
            parts.append(((nn(high, block) + nn(low, block)) * live).astype(BF16))
        turned = jnp.concatenate(parts, axis=0)
        column = jnp.concatenate(
            [arrived[s * (share + 1) + f] for s in range(peers)], axis=0
        )
        flipped = column.astype(F32).T.astype(BF16)
        whitened = nt(flipped, turned).astype(BF16)
        gram = gram + nt(whitened, whitened)
        mine = iota2(8, 128, 0) == f % 8
        high, low = split(jnp.where(mine, b[:, 128 * (f // 8) : 128 * (f // 8) + 128] * live, 0.0))
        pull = pull + (nn(high, column) + nn(low, column))
    out[0:16] = gram[0:128, 0:128].reshape(16, 8, 128)
    out[16:32] = gram[128:256, 0:128].reshape(16, 8, 128)
    out[32:48] = gram[128:256, 128:256].reshape(16, 8, 128)
    total = jnp.sum(pull, axis=0, keepdims=True)
    last = jnp.concatenate(
        [total[:, 0:128], total[:, 128:256], jnp.zeros((6, 128), F32)], axis=0
    )
    out[48:64] = jnp.zeros((16, 8, 128), F32)
    out[48] = last


def lower_half(x):
    i, j = iota2(MEM, MEM, 0), iota2(MEM, MEM, 1)
    return jnp.where(i > j, x, jnp.where(i == j, 0.5 * x, 0.0))


def solve_kernel(summed, basis, out, system, inverse, rows):
    eye = (iota2(MEM, MEM, 0) == iota2(MEM, MEM, 1)).astype(F32)
    g00 = summed[0:16].reshape(128, 128)
    g10 = summed[16:32].reshape(128, 128)
    g11 = summed[32:48].reshape(128, 128)
    a = jnp.concatenate(
        [jnp.concatenate([g00, g10.T], axis=1), jnp.concatenate([g10, g11], axis=1)], axis=0
    ) + (MEM - 1.0) * eye
    system[...] = a
    across = lax.rsqrt(jnp.sum(a * eye, axis=0, keepdims=True))
    down = lax.rsqrt(jnp.sum(a * eye, axis=1, keepdims=True))
    x = across * (eye - lower_half(a * across * down - eye))
    residual = nt(nn(x, a), x) - eye
    inverse[...] = x - nn(lower_half(residual), x)

    def go_on(state):
        step, size = state
        return jnp.logical_and(step < 9, jnp.logical_and(size >= 1e-4, size < 1e6))

    def refine(state):
        step, _ = state
        x = inverse[...]
        residual = nt(nn(x, system[...], HI), x, HI) - eye
        inverse[...] = x - nn(lower_half(residual), x, HI)
        return step + 1, jnp.sum(residual * residual)

    _, size = lax.while_loop(go_on, refine, (jnp.int32(0), jnp.float32(1.0)))

    @pl.when(jnp.logical_not(size < 1e-4))
    def _():
        rows[:, 0:MEM] = system[...]
        rows[:, MEM : 2 * MEM] = eye
        lanes = iota2(1, 2 * MEM, 1)

        def eliminate(j, carry):
            row = rows[pl.ds(j, 1), :]
            pivot = jnp.sum(jnp.where(lanes == j, row, 0.0), axis=1, keepdims=True)
            old = rows[...]
            column = jnp.sum(jnp.where(lanes == j, old, 0.0), axis=1, keepdims=True)
            below = iota2(MEM, 1, 0) > j
            rows[...] = old - jnp.where(below, column / pivot, 0.0) * row
            rows[pl.ds(j, 1), :] = row * (1.0 / jnp.sqrt(pivot))
            return carry

        lax.fori_loop(0, MEM, eliminate, 0)
        inverse[...] = rows[:, MEM : 2 * MEM]

    x = inverse[...]
    last = summed[48]
    pull = jnp.concatenate([last[0:1, :], last[1:2, :]], axis=1)
    halfway = nt(x, jnp.broadcast_to(pull, (MEM, MEM)), HI)
    target = (MEM - 1.0) ** 0.5 * basis[...] + halfway
    out[...] = nn(x.T, target, HI).astype(BF16)


def send_by(value, axis, steps):
    count = lax.axis_size(axis)
    return lax.ppermute(value, axis, [(s, (s + steps) % count) for s in range(count)])


def swap(x, axis):
    return lax.all_to_all(x, axis, 0, 0, tiled=True)


def summed_everywhere(tiles):
    mine = jnp.sum(swap(tiles, NEAR), axis=0, keepdims=True)
    far = lax.axis_size(FAR)
    mine = jnp.sum(swap(jnp.broadcast_to(mine, (far, 8, 128)), FAR), axis=0, keepdims=True)
    return swap(jnp.broadcast_to(mine, (tiles.shape[0], 8, 128)), NEAR)


def local(
    ensemble,
    jacobian,
    innovation,
    error_vectors,
    error_values,
    ensemble_vectors,
    column_pick,
    footprint_slot,
    footprint_count,
):
    window, capacity = column_pick.shape[1:]
    levels, members = ensemble.shape[1:]
    width = error_vectors.shape[1]
    foot_rows = jacobian.shape[0]
    peers = lax.axis_size(CHAN)
    share = foot_rows // peers
    slab = (levels, members)

    sensitivity = swap(jacobian, CHAN)

    chosen = pl.pallas_call(
        pick_kernel,
        out_shape=[jax.ShapeDtypeStruct((capacity, *slab), BF16)] * window,
        in_specs=[SM, VM],
        out_specs=[VM] * window,
        compiler_params=PARAMS,
        cost_estimate=cost(0, 2 * ensemble.size),
        name="pick",
    )(column_pick.reshape(-1), ensemble)
    parts = []
    for o in range(window):
        steps = o - window // 2
        parts.append(send_by(chosen[o], TILE, steps) if steps else chosen[o])

    place = jnp.concatenate(
        [lax.axis_index(CHAN).astype(jnp.int32)[None], footprint_count.astype(jnp.int32)]
    )
    slabs = pl.pallas_call(
        weights_kernel,
        out_shape=jax.ShapeDtypeStruct((peers, *slab), BF16),
        in_specs=[SM, VM, VM, VM, VM],
        out_specs=VM,
        scratch_shapes=[pltpu.VMEM((foot_rows, 128), F32)],
        compiler_params=PARAMS,
        cost_estimate=cost(2 * foot_rows * 256 * 128, 2 * jacobian.size),
        name="weights",
    )(place, innovation, error_vectors, 1.0 / error_values.reshape(peers, width), jacobian)

    payload = pl.pallas_call(
        slot_kernel,
        out_shape=jax.ShapeDtypeStruct((foot_rows + peers, *slab), BF16),
        in_specs=[SM] + [VM] * (window + 1),
        out_specs=VM,
        scratch_shapes=[pltpu.VMEM((window * capacity, *slab), BF16)],
        compiler_params=PARAMS,
        cost_estimate=cost(0, 4 * foot_rows * levels * members),
        name="slots",
    )(footprint_slot, *parts, slabs)
    arrived = swap(payload, CHAN)

    tiles = pl.pallas_call(
        terms_kernel,
        out_shape=jax.ShapeDtypeStruct((64, 8, 128), F32),
        in_specs=[SM, VM, VM, VM, VM],
        out_specs=VM,
        compiler_params=PARAMS,
        cost_estimate=cost(4 * 512 * share * 256 * 384, 2 * jacobian.size),
        name="terms",
    )(place, error_vectors, 1.0 / jnp.sqrt(error_values).reshape(2, members), sensitivity, arrived)

    summed = summed_everywhere(tiles)

    transform = pl.pallas_call(
        solve_kernel,
        out_shape=jax.ShapeDtypeStruct((members, members), BF16),
        in_specs=[VM, VM],
        out_specs=VM,
        scratch_shapes=[
            pltpu.VMEM((members, members), F32),
            pltpu.VMEM((members, members), F32),
            pltpu.VMEM((members, 2 * members), F32),
        ],
        compiler_params=PARAMS,
        name="solve",
    )(summed, ensemble_vectors)

    updated = jnp.dot(
        ensemble.reshape(-1, members), transform, preferred_element_type=F32
    ).astype(BF16)
    return updated.reshape(ensemble.shape)


def solution(mesh):
    finer = Mesh(mesh.devices.reshape(8, 4, 8, 2), ("y", "x", "z", "c"))
    return jax.shard_map(
        local,
        mesh=finer,
        in_specs=(
            P(TILE, CHAN, None),
            P(TILE, CHAN, None),
            P(TILE, CHAN),
            P(),
            P(),
            P(),
            P(TILE, None, None),
            P(TILE),
            P(TILE),
        ),
        out_specs=P(TILE, CHAN, None),
        check_vma=False,
    )
```

```python
import jax
import jax.numpy as jnp
from jax import lax
from jax.experimental import pallas as pl
from jax.experimental.pallas import tpu as pltpu
from jax.sharding import Mesh
from jax.sharding import PartitionSpec as P

TILE = ("y", "x")
CHAN = ("z", "c")
NEAR = ("x", "z", "c")
FAR = "y"
MEM = 256
HI = lax.Precision.HIGHEST
F32 = jnp.float32
BF16 = jnp.bfloat16
VM = pl.BlockSpec(memory_space=pltpu.VMEM)
SM = pl.BlockSpec(memory_space=pltpu.SMEM)
PARAMS = pltpu.CompilerParams(vmem_limit_bytes=48 * 2**20)


def cost(flops, size):
    return pl.CostEstimate(flops=flops, bytes_accessed=size, transcendentals=0)


def iota2(rows, columns, dim):
    return lax.broadcasted_iota(jnp.int32, (rows, columns), dim)


def nt(a, b, precision=None):
    return lax.dot_general(
        a, b, (((1,), (1,)), ((), ())), precision=precision, preferred_element_type=F32
    )


def nn(a, b, precision=None):
    return lax.dot_general(
        a, b, (((1,), (0,)), ((), ())), precision=precision, preferred_element_type=F32
    )


def split(x):
    high = x.astype(BF16)
    return high, (x - high.astype(F32)).astype(BF16)


def pick_kernel(pick, ensemble, *sends):
    capacity = sends[0].shape[0]
    for o, out in enumerate(sends):

        def one(j, carry, o=o, out=out):
            out[j] = ensemble[pick[o * capacity + j]]
            return carry

        lax.fori_loop(0, capacity, one, 0, unroll=8)


def weights_kernel(place, innovation, vectors, inverses, jacobian, slabs, sums):
    group = place[0]
    width = vectors.shape[1]
    start = pl.multiple_of(group * width, width)
    basis = vectors[pl.ds(start, width), :]
    scaled = basis * inverses[pl.ds(group, 1), :]
    tiled = nt(scaled, jnp.concatenate([basis] * 8, axis=0), HI)
    weights = nn(innovation[...], tiled, HI)
    mine = iota2(8, 8 * width, 1) // width == iota2(8, 8 * width, 0)
    rows = innovation.shape[0]
    for k in range(rows // 8):
        high, low = split(jnp.where(mine, weights[8 * k : 8 * k + 8], 0.0))
        block = jacobian[8 * k : 8 * k + 8].reshape(8 * width, 128)
        sums[8 * k : 8 * k + 8, :] = nn(high, block) + nn(low, block)
    share = rows // slabs.shape[0]
    zero = jnp.zeros((8 - (share - 8), 128), F32)
    for i in range(slabs.shape[0]):
        left = sums[share * i : share * i + 8, :]
        right = jnp.concatenate([sums[share * i + 8 : share * i + share, :], zero], axis=0)
        slabs[i] = jnp.concatenate([left, right], axis=1).astype(BF16)


def slot_kernel(slot, a0, a1, a2, a3, a4, slabs, out, held):
    capacity = a0.shape[0]
    for o, part in enumerate((a0, a1, a2, a3, a4)):
        held[o * capacity : (o + 1) * capacity] = part[...]
    peers = slabs.shape[0]
    share = out.shape[0] // peers - 1

    def one(i, carry):
        for f in range(share):
            out[i * (share + 1) + f] = held[slot[i * share + f]]
        out[i * (share + 1) + share] = slabs[i]
        return carry

    lax.fori_loop(0, peers, one, 0)


def terms_kernel(place, vectors, scales, jacobian, arrived, out):
    peers = vectors.shape[0] // vectors.shape[1]
    share = jacobian.shape[0] // peers
    first = place[0] * share
    count = place[1]
    half = MEM
    same = iota2(half, half, 0) // 32 == iota2(half, half, 1) // 32
    turns = []
    for h in range(2):
        block = vectors[h * half : (h + 1) * half, :]
        wide = jnp.where(same, jnp.concatenate([block] * 8, axis=1), 0.0) * scales[h : h + 1, :]
        turns.append(split(wide.T))
    b = arrived[share].astype(F32)
    for source in range(1, peers):
        b = b + arrived[source * (share + 1) + share].astype(F32)
    gram = jnp.zeros((MEM, MEM), F32)
    pull = jnp.zeros((8, MEM), F32)
    for f in range(share):
        live = jnp.where(first + f < count, 1.0, 0.0).astype(F32)
        parts = []
        for h in range(2):
            block = jnp.concatenate(
                [jacobian[(h * 8 + s) * share + f] for s in range(8)], axis=0
            )
            high, low = turns[h]
            parts.append(((nn(high, block) + nn(low, block)) * live).astype(BF16))
        turned = jnp.concatenate(parts, axis=0)
        column = jnp.concatenate(
            [arrived[s * (share + 1) + f] for s in range(peers)], axis=0
        )
        flipped = column.astype(F32).T.astype(BF16)
        whitened = nt(flipped, turned).astype(BF16)
        gram = gram + nt(whitened, whitened)
        mine = iota2(8, 128, 0) == f % 8
        high, low = split(jnp.where(mine, b[:, 128 * (f // 8) : 128 * (f // 8) + 128] * live, 0.0))
        pull = pull + (nn(high, column) + nn(low, column))
    out[0:16] = gram[0:128, 0:128].reshape(16, 8, 128)
    out[16:32] = gram[128:256, 0:128].reshape(16, 8, 128)
    out[32:48] = gram[128:256, 128:256].reshape(16, 8, 128)
    total = jnp.sum(pull, axis=0, keepdims=True)
    last = jnp.concatenate(
        [total[:, 0:128], total[:, 128:256], jnp.zeros((6, 128), F32)], axis=0
    )
    out[48:64] = jnp.zeros((16, 8, 128), F32)
    out[48] = last


def lower_half(x):
    i, j = iota2(MEM, MEM, 0), iota2(MEM, MEM, 1)
    return jnp.where(i > j, x, jnp.where(i == j, 0.5 * x, 0.0))


def solve_kernel(summed, basis, ensemble, out, system, inverse, rows, held, sems):
    eye = (iota2(MEM, MEM, 0) == iota2(MEM, MEM, 1)).astype(F32)
    g00 = summed[0:16].reshape(128, 128)
    g10 = summed[16:32].reshape(128, 128)
    g11 = summed[32:48].reshape(128, 128)
    a = jnp.concatenate(
        [jnp.concatenate([g00, g10.T], axis=1), jnp.concatenate([g10, g11], axis=1)], axis=0
    ) + (MEM - 1.0) * eye
    system[...] = a
    across = lax.rsqrt(jnp.sum(a * eye, axis=0, keepdims=True))
    down = lax.rsqrt(jnp.sum(a * eye, axis=1, keepdims=True))
    x = across * (eye - lower_half(a * across * down - eye))
    residual = nt(nn(x, a), x) - eye
    inverse[...] = x - nn(lower_half(residual), x)

    def go_on(state):
        step, size = state
        return jnp.logical_and(step < 9, jnp.logical_and(size >= 1e-4, size < 1e6))

    def refine(state):
        step, _ = state
        x = inverse[...]
        residual = nt(nn(x, system[...], HI), x, HI) - eye
        inverse[...] = x - nn(lower_half(residual), x, HI)
        return step + 1, jnp.sum(residual * residual)

    _, size = lax.while_loop(go_on, refine, (jnp.int32(0), jnp.float32(1.0)))

    @pl.when(jnp.logical_not(size < 1e-4))
    def _():
        rows[:, 0:MEM] = system[...]
        rows[:, MEM : 2 * MEM] = eye
        lanes = iota2(1, 2 * MEM, 1)

        def eliminate(j, carry):
            row = rows[pl.ds(j, 1), :]
            pivot = jnp.sum(jnp.where(lanes == j, row, 0.0), axis=1, keepdims=True)
            old = rows[...]
            column = jnp.sum(jnp.where(lanes == j, old, 0.0), axis=1, keepdims=True)
            below = iota2(MEM, 1, 0) > j
            rows[...] = old - jnp.where(below, column / pivot, 0.0) * row
            rows[pl.ds(j, 1), :] = row * (1.0 / jnp.sqrt(pivot))
            return carry

        lax.fori_loop(0, MEM, eliminate, 0)
        inverse[...] = rows[:, MEM : 2 * MEM]

    x = inverse[...]
    last = summed[48]
    pull = jnp.concatenate([last[0:1, :], last[1:2, :]], axis=1)
    halfway = nt(x, jnp.broadcast_to(pull, (MEM, MEM)), HI)
    target = (MEM - 1.0) ** 0.5 * basis[...] + halfway
    transform = nn(x.T, target, HI).astype(BF16)
    copies = []
    for i in range(held.shape[0]):
        size = held.shape[1]
        held[i] = nn(ensemble[i * size : (i + 1) * size, :], transform).astype(BF16)
        copies.append(
            pltpu.make_async_copy(held.at[i], out.at[i * size : (i + 1) * size], sems.at[i])
        )
        copies[-1].start()
    for copy in copies:
        copy.wait()


def send_by(value, axis, steps):
    count = lax.axis_size(axis)
    return lax.ppermute(value, axis, [(s, (s + steps) % count) for s in range(count)])


def swap(x, axis):
    return lax.all_to_all(x, axis, 0, 0, tiled=True)


def summed_everywhere(tiles):
    mine = jnp.sum(swap(tiles, NEAR), axis=0, keepdims=True)
    far = lax.axis_size(FAR)
    mine = jnp.sum(swap(jnp.broadcast_to(mine, (far, 8, 128)), FAR), axis=0, keepdims=True)
    return swap(jnp.broadcast_to(mine, (tiles.shape[0], 8, 128)), NEAR)


def local(
    ensemble,
    jacobian,
    innovation,
    error_vectors,
    error_values,
    ensemble_vectors,
    column_pick,
    footprint_slot,
    footprint_count,
):
    window, capacity = column_pick.shape[1:]
    levels, members = ensemble.shape[1:]
    width = error_vectors.shape[1]
    foot_rows = jacobian.shape[0]
    peers = lax.axis_size(CHAN)
    share = foot_rows // peers
    slab = (levels, members)

    sensitivity = swap(jacobian, CHAN)

    chosen = pl.pallas_call(
        pick_kernel,
        out_shape=[jax.ShapeDtypeStruct((capacity, *slab), BF16)] * window,
        in_specs=[SM, VM],
        out_specs=[VM] * window,
        compiler_params=PARAMS,
        cost_estimate=cost(0, 2 * ensemble.size),
        name="pick",
    )(column_pick.reshape(-1), ensemble)
    parts = []
    for o in range(window):
        steps = o - window // 2
        parts.append(send_by(chosen[o], TILE, steps) if steps else chosen[o])

    place = jnp.concatenate(
        [lax.axis_index(CHAN).astype(jnp.int32)[None], footprint_count.astype(jnp.int32)]
    )
    slabs = pl.pallas_call(
        weights_kernel,
        out_shape=jax.ShapeDtypeStruct((peers, *slab), BF16),
        in_specs=[SM, VM, VM, VM, VM],
        out_specs=VM,
        scratch_shapes=[pltpu.VMEM((foot_rows, 128), F32)],
        compiler_params=PARAMS,
        cost_estimate=cost(2 * foot_rows * 256 * 128, 2 * jacobian.size),
        name="weights",
    )(place, innovation, error_vectors, 1.0 / error_values.reshape(peers, width), jacobian)

    payload = pl.pallas_call(
        slot_kernel,
        out_shape=jax.ShapeDtypeStruct((foot_rows + peers, *slab), BF16),
        in_specs=[SM] + [VM] * (window + 1),
        out_specs=VM,
        scratch_shapes=[pltpu.VMEM((window * capacity, *slab), BF16)],
        compiler_params=PARAMS,
        cost_estimate=cost(0, 4 * foot_rows * levels * members),
        name="slots",
    )(footprint_slot, *parts, slabs)
    payload, sensitivity = lax.optimization_barrier((payload, sensitivity))
    arrived = swap(payload, CHAN)

    tiles = pl.pallas_call(
        terms_kernel,
        out_shape=jax.ShapeDtypeStruct((64, 8, 128), F32),
        in_specs=[SM, VM, VM, VM, VM],
        out_specs=VM,
        compiler_params=PARAMS,
        cost_estimate=cost(4 * 512 * share * 256 * 384, 2 * jacobian.size),
        name="terms",
    )(place, error_vectors, 1.0 / jnp.sqrt(error_values).reshape(2, members), sensitivity, arrived)

    summed = summed_everywhere(tiles)

    chunks = 6
    flat_rows = ensemble.reshape(-1, members)
    updated = pl.pallas_call(
        solve_kernel,
        out_shape=jax.ShapeDtypeStruct(flat_rows.shape, BF16),
        in_specs=[VM, VM, VM],
        out_specs=pl.BlockSpec(memory_space=pl.ANY),
        scratch_shapes=[
            pltpu.VMEM((members, members), F32),
            pltpu.VMEM((members, members), F32),
            pltpu.VMEM((members, 2 * members), F32),
            pltpu.VMEM((chunks, flat_rows.shape[0] // chunks, members), BF16),
            pltpu.SemaphoreType.DMA((chunks,)),
        ],
        compiler_params=PARAMS,
        name="solve",
    )(summed, ensemble_vectors, flat_rows)
    return updated.reshape(ensemble.shape)


def solution(mesh):
    finer = Mesh(mesh.devices.reshape(8, 4, 8, 2), ("y", "x", "z", "c"))
    return jax.shard_map(
        local,
        mesh=finer,
        in_specs=(
            P(TILE, CHAN, None),
            P(TILE, CHAN, None),
            P(TILE, CHAN),
            P(),
            P(),
            P(),
            P(TILE, None, None),
            P(TILE),
            P(TILE),
        ),
        out_specs=P(TILE, CHAN, None),
        check_vma=False,
    )
```

```python
import jax
import jax.numpy as jnp
from jax import lax
from jax.experimental import pallas as pl
from jax.experimental.pallas import tpu as pltpu
from jax.sharding import Mesh
from jax.sharding import PartitionSpec as P

TILE = ("y", "x")
CHAN = ("z", "c")
NEAR = ("x", "z", "c")
FAR = "y"
MEM = 256
HI = lax.Precision.HIGHEST
F32 = jnp.float32
BF16 = jnp.bfloat16
VM = pl.BlockSpec(memory_space=pltpu.VMEM)
SM = pl.BlockSpec(memory_space=pltpu.SMEM)
PARAMS = pltpu.CompilerParams(vmem_limit_bytes=48 * 2**20)


def cost(flops, size):
    return pl.CostEstimate(flops=flops, bytes_accessed=size, transcendentals=0)


def iota2(rows, columns, dim):
    return lax.broadcasted_iota(jnp.int32, (rows, columns), dim)


def nt(a, b, precision=None):
    return lax.dot_general(
        a, b, (((1,), (1,)), ((), ())), precision=precision, preferred_element_type=F32
    )


def nn(a, b, precision=None):
    return lax.dot_general(
        a, b, (((1,), (0,)), ((), ())), precision=precision, preferred_element_type=F32
    )


def split(x):
    high = x.astype(BF16)
    return high, (x - high.astype(F32)).astype(BF16)


def pick_kernel(pick, ensemble, *sends):
    capacity = sends[0].shape[0]
    for o, out in enumerate(sends):

        def one(j, carry, o=o, out=out):
            out[j] = ensemble[pick[o * capacity + j]]
            return carry

        lax.fori_loop(0, capacity, one, 0, unroll=8)


def weights_kernel(place, innovation, vectors, inverses, jacobian, slabs, sums):
    group = place[0]
    width = vectors.shape[1]
    start = pl.multiple_of(group * width, width)
    basis = vectors[pl.ds(start, width), :]
    scaled = basis * inverses[pl.ds(group, 1), :]
    tiled = nt(scaled, jnp.concatenate([basis] * 8, axis=0), HI)
    weights = nn(innovation[...], tiled, HI)
    mine = iota2(8, 8 * width, 1) // width == iota2(8, 8 * width, 0)
    rows = innovation.shape[0]
    for k in range(rows // 8):
        high, low = split(jnp.where(mine, weights[8 * k : 8 * k + 8], 0.0))
        block = jacobian[8 * k : 8 * k + 8].reshape(8 * width, 128)
        sums[8 * k : 8 * k + 8, :] = nn(high, block) + nn(low, block)
    share = rows // slabs.shape[0]
    zero = jnp.zeros((8 - (share - 8), 128), F32)
    for i in range(slabs.shape[0]):
        left = sums[share * i : share * i + 8, :]
        right = jnp.concatenate([sums[share * i + 8 : share * i + share, :], zero], axis=0)
        slabs[i] = jnp.concatenate([left, right], axis=1).astype(BF16)


def slot_kernel(slot, a0, a1, a2, a3, a4, slabs, out, held):
    capacity = a0.shape[0]
    for o, part in enumerate((a0, a1, a2, a3, a4)):
        held[o * capacity : (o + 1) * capacity] = part[...]
    peers = slabs.shape[0]
    share = out.shape[0] // peers - 1

    def one(i, carry):
        for f in range(share):
            out[i * (share + 1) + f] = held[slot[i * share + f]]
        out[i * (share + 1) + share] = slabs[i]
        return carry

    lax.fori_loop(0, peers, one, 0)


def turn_kernel(place, vectors, scales, jacobian, out):
    peers = vectors.shape[0] // vectors.shape[1]
    share = jacobian.shape[0] // peers
    first = place[0] * share
    count = place[1]
    half = MEM
    same = iota2(half, half, 0) // 32 == iota2(half, half, 1) // 32
    turns = []
    for h in range(2):
        block = vectors[h * half : (h + 1) * half, :]
        wide = jnp.where(same, jnp.concatenate([block] * 8, axis=1), 0.0) * scales[h : h + 1, :]
        turns.append(split(wide.T))
    for f in range(share):
        live = jnp.where(first + f < count, 1.0, 0.0).astype(F32)
        for h in range(2):
            block = jnp.concatenate(
                [jacobian[(h * 8 + s) * share + f] for s in range(8)], axis=0
            )
            high, low = turns[h]
            turned = (nn(high, block) + nn(low, block)) * live
            out[f, h * half : (h + 1) * half, :] = turned.astype(BF16)


def terms_kernel(place, turned, arrived, out):
    share = turned.shape[0]
    peers = arrived.shape[0] // (share + 1)
    first = place[0] * share
    count = place[1]
    b = arrived[share].astype(F32)
    for source in range(1, peers):
        b = b + arrived[source * (share + 1) + share].astype(F32)
    gram = jnp.zeros((MEM, MEM), F32)
    pull = jnp.zeros((8, MEM), F32)
    for f in range(share):
        live = jnp.where(first + f < count, 1.0, 0.0).astype(F32)
        column = jnp.concatenate(
            [arrived[s * (share + 1) + f] for s in range(peers)], axis=0
        )
        flipped = column.astype(F32).T.astype(BF16)
        whitened = nt(flipped, turned[f]).astype(BF16)
        gram = gram + nt(whitened, whitened)
        mine = iota2(8, 128, 0) == f % 8
        high, low = split(jnp.where(mine, b[:, 128 * (f // 8) : 128 * (f // 8) + 128] * live, 0.0))
        pull = pull + (nn(high, column) + nn(low, column))
    out[0:16] = gram[0:128, 0:128].reshape(16, 8, 128)
    out[16:32] = gram[128:256, 0:128].reshape(16, 8, 128)
    out[32:48] = gram[128:256, 128:256].reshape(16, 8, 128)
    total = jnp.sum(pull, axis=0, keepdims=True)
    last = jnp.concatenate(
        [total[:, 0:128], total[:, 128:256], jnp.zeros((6, 128), F32)], axis=0
    )
    out[48:64] = jnp.zeros((16, 8, 128), F32)
    out[48] = last


def lower_half(x):
    i, j = iota2(MEM, MEM, 0), iota2(MEM, MEM, 1)
    return jnp.where(i > j, x, jnp.where(i == j, 0.5 * x, 0.0))


def solve_kernel(summed, basis, ensemble, out, system, inverse, rows, held, sems):
    eye = (iota2(MEM, MEM, 0) == iota2(MEM, MEM, 1)).astype(F32)
    g00 = summed[0:16].reshape(128, 128)
    g10 = summed[16:32].reshape(128, 128)
    g11 = summed[32:48].reshape(128, 128)
    a = jnp.concatenate(
        [jnp.concatenate([g00, g10.T], axis=1), jnp.concatenate([g10, g11], axis=1)], axis=0
    ) + (MEM - 1.0) * eye
    system[...] = a
    across = lax.rsqrt(jnp.sum(a * eye, axis=0, keepdims=True))
    down = lax.rsqrt(jnp.sum(a * eye, axis=1, keepdims=True))
    x = across * (eye - lower_half(a * across * down - eye))
    residual = nt(nn(x, a), x) - eye
    inverse[...] = x - nn(lower_half(residual), x)

    def go_on(state):
        step, size = state
        return jnp.logical_and(step < 9, jnp.logical_and(size >= 1e-4, size < 1e6))

    def refine(state):
        step, _ = state
        x = inverse[...]
        residual = nt(nn(x, system[...], HI), x, HI) - eye
        inverse[...] = x - nn(lower_half(residual), x, HI)
        return step + 1, jnp.sum(residual * residual)

    _, size = lax.while_loop(go_on, refine, (jnp.int32(0), jnp.float32(1.0)))

    @pl.when(jnp.logical_not(size < 1e-4))
    def _():
        rows[:, 0:MEM] = system[...]
        rows[:, MEM : 2 * MEM] = eye
        lanes = iota2(1, 2 * MEM, 1)

        def eliminate(j, carry):
            row = rows[pl.ds(j, 1), :]
            pivot = jnp.sum(jnp.where(lanes == j, row, 0.0), axis=1, keepdims=True)
            old = rows[...]
            column = jnp.sum(jnp.where(lanes == j, old, 0.0), axis=1, keepdims=True)
            below = iota2(MEM, 1, 0) > j
            rows[...] = old - jnp.where(below, column / pivot, 0.0) * row
            rows[pl.ds(j, 1), :] = row * (1.0 / jnp.sqrt(pivot))
            return carry

        lax.fori_loop(0, MEM, eliminate, 0)
        inverse[...] = rows[:, MEM : 2 * MEM]

    x = inverse[...]
    last = summed[48]
    pull = jnp.concatenate([last[0:1, :], last[1:2, :]], axis=1)
    halfway = nt(x, jnp.broadcast_to(pull, (MEM, MEM)), HI)
    target = (MEM - 1.0) ** 0.5 * basis[...] + halfway
    transform = nn(x.T, target, HI).astype(BF16)
    copies = []
    for i in range(held.shape[0]):
        size = held.shape[1]
        held[i] = nn(ensemble[i * size : (i + 1) * size, :], transform).astype(BF16)
        copies.append(
            pltpu.make_async_copy(held.at[i], out.at[i * size : (i + 1) * size], sems.at[i])
        )
        copies[-1].start()
    for copy in copies:
        copy.wait()


def send_by(value, axis, steps):
    count = lax.axis_size(axis)
    return lax.ppermute(value, axis, [(s, (s + steps) % count) for s in range(count)])


def swap(x, axis):
    return lax.all_to_all(x, axis, 0, 0, tiled=True)


def summed_everywhere(tiles):
    mine = jnp.sum(swap(tiles, NEAR), axis=0, keepdims=True)
    far = lax.axis_size(FAR)
    mine = jnp.sum(swap(jnp.broadcast_to(mine, (far, 8, 128)), FAR), axis=0, keepdims=True)
    return swap(jnp.broadcast_to(mine, (tiles.shape[0], 8, 128)), NEAR)


def local(
    ensemble,
    jacobian,
    innovation,
    error_vectors,
    error_values,
    ensemble_vectors,
    column_pick,
    footprint_slot,
    footprint_count,
):
    window, capacity = column_pick.shape[1:]
    levels, members = ensemble.shape[1:]
    width = error_vectors.shape[1]
    foot_rows = jacobian.shape[0]
    peers = lax.axis_size(CHAN)
    share = foot_rows // peers
    slab = (levels, members)

    sensitivity = swap(jacobian, CHAN)

    chosen = pl.pallas_call(
        pick_kernel,
        out_shape=[jax.ShapeDtypeStruct((capacity, *slab), BF16)] * window,
        in_specs=[SM, VM],
        out_specs=[VM] * window,
        compiler_params=PARAMS,
        cost_estimate=cost(0, 2 * ensemble.size),
        name="pick",
    )(column_pick.reshape(-1), ensemble)
    parts = []
    for o in range(window):
        steps = o - window // 2
        parts.append(send_by(chosen[o], TILE, steps) if steps else chosen[o])

    place = jnp.concatenate(
        [lax.axis_index(CHAN).astype(jnp.int32)[None], footprint_count.astype(jnp.int32)]
    )
    slabs = pl.pallas_call(
        weights_kernel,
        out_shape=jax.ShapeDtypeStruct((peers, *slab), BF16),
        in_specs=[SM, VM, VM, VM, VM],
        out_specs=VM,
        scratch_shapes=[pltpu.VMEM((foot_rows, 128), F32)],
        compiler_params=PARAMS,
        cost_estimate=cost(2 * foot_rows * 256 * 128, 2 * jacobian.size),
        name="weights",
    )(place, innovation, error_vectors, 1.0 / error_values.reshape(peers, width), jacobian)

    payload = pl.pallas_call(
        slot_kernel,
        out_shape=jax.ShapeDtypeStruct((foot_rows + peers, *slab), BF16),
        in_specs=[SM] + [VM] * (window + 1),
        out_specs=VM,
        scratch_shapes=[pltpu.VMEM((window * capacity, *slab), BF16)],
        compiler_params=PARAMS,
        cost_estimate=cost(0, 4 * foot_rows * levels * members),
        name="slots",
    )(footprint_slot, *parts, slabs)
    payload, sensitivity = lax.optimization_barrier((payload, sensitivity))
    arrived = swap(payload, CHAN)

    turned = pl.pallas_call(
        turn_kernel,
        out_shape=jax.ShapeDtypeStruct((share, peers * width, 128), BF16),
        in_specs=[SM, VM, VM, VM],
        out_specs=VM,
        compiler_params=PARAMS,
        cost_estimate=cost(4 * 512 * share * 256 * 128, 4 * jacobian.size),
        name="turn",
    )(place, error_vectors, 1.0 / jnp.sqrt(error_values).reshape(2, members), sensitivity)

    tiles = pl.pallas_call(
        terms_kernel,
        out_shape=jax.ShapeDtypeStruct((64, 8, 128), F32),
        in_specs=[SM, VM, VM],
        out_specs=VM,
        compiler_params=PARAMS,
        cost_estimate=cost(2 * 512 * share * 256 * 384, 2 * jacobian.size),
        name="terms",
    )(place, turned, arrived)

    summed = summed_everywhere(tiles)

    chunks = 6
    flat_rows = ensemble.reshape(-1, members)
    updated = pl.pallas_call(
        solve_kernel,
        out_shape=jax.ShapeDtypeStruct(flat_rows.shape, BF16),
        in_specs=[VM, VM, VM],
        out_specs=pl.BlockSpec(memory_space=pl.ANY),
        scratch_shapes=[
            pltpu.VMEM((members, members), F32),
            pltpu.VMEM((members, members), F32),
            pltpu.VMEM((members, 2 * members), F32),
            pltpu.VMEM((chunks, flat_rows.shape[0] // chunks, members), BF16),
            pltpu.SemaphoreType.DMA((chunks,)),
        ],
        compiler_params=PARAMS,
        name="solve",
    )(summed, ensemble_vectors, flat_rows)
    return updated.reshape(ensemble.shape)


def solution(mesh):
    finer = Mesh(mesh.devices.reshape(8, 4, 8, 2), ("y", "x", "z", "c"))
    return jax.shard_map(
        local,
        mesh=finer,
        in_specs=(
            P(TILE, CHAN, None),
            P(TILE, CHAN, None),
            P(TILE, CHAN),
            P(),
            P(),
            P(),
            P(TILE, None, None),
            P(TILE),
            P(TILE),
        ),
        out_specs=P(TILE, CHAN, None),
        check_vma=False,
    )
```

```python
import jax
import jax.numpy as jnp
from jax import lax
from jax.experimental import pallas as pl
from jax.experimental.pallas import tpu as pltpu
from jax.sharding import Mesh
from jax.sharding import PartitionSpec as P

TILE = ("y", "x")
CHAN = ("z", "c")
NEAR = ("x", "z")
FAR = "y"
CORE = "c"
MEM = 256
HI = lax.Precision.HIGHEST
F32 = jnp.float32
BF16 = jnp.bfloat16
VM = pl.BlockSpec(memory_space=pltpu.VMEM)
SM = pl.BlockSpec(memory_space=pltpu.SMEM)
PARAMS = pltpu.CompilerParams(vmem_limit_bytes=48 * 2**20)


def cost(flops, size):
    return pl.CostEstimate(flops=flops, bytes_accessed=size, transcendentals=0)


def iota2(rows, columns, dim):
    return lax.broadcasted_iota(jnp.int32, (rows, columns), dim)


def nt(a, b, precision=None):
    return lax.dot_general(
        a, b, (((1,), (1,)), ((), ())), precision=precision, preferred_element_type=F32
    )


def nn(a, b, precision=None):
    return lax.dot_general(
        a, b, (((1,), (0,)), ((), ())), precision=precision, preferred_element_type=F32
    )


def split(x):
    high = x.astype(BF16)
    return high, (x - high.astype(F32)).astype(BF16)


def pick_kernel(pick, ensemble, *sends):
    capacity = sends[0].shape[0]
    for o, out in enumerate(sends):

        def one(j, carry, o=o, out=out):
            out[j] = ensemble[pick[o * capacity + j]]
            return carry

        lax.fori_loop(0, capacity, one, 0, unroll=8)


def weights_kernel(place, innovation, vectors, inverses, jacobian, slabs, sums):
    group = place[0]
    width = vectors.shape[1]
    start = pl.multiple_of(group * width, width)
    basis = vectors[pl.ds(start, width), :]
    scaled = basis * inverses[pl.ds(group, 1), :]
    tiled = nt(scaled, jnp.concatenate([basis] * 8, axis=0), HI)
    weights = nn(innovation[...], tiled, HI)
    mine = iota2(8, 8 * width, 1) // width == iota2(8, 8 * width, 0)
    rows = innovation.shape[0]
    for k in range(rows // 8):
        high, low = split(jnp.where(mine, weights[8 * k : 8 * k + 8], 0.0))
        block = jacobian[8 * k : 8 * k + 8].reshape(8 * width, 128)
        sums[8 * k : 8 * k + 8, :] = nn(high, block) + nn(low, block)
    share = rows // slabs.shape[0]
    zero = jnp.zeros((8 - (share - 8), 128), F32)
    for i in range(slabs.shape[0]):
        left = sums[share * i : share * i + 8, :]
        right = jnp.concatenate([sums[share * i + 8 : share * i + share, :], zero], axis=0)
        slabs[i] = jnp.concatenate([left, right], axis=1).astype(BF16)


def slot_kernel(slot, a0, a1, a2, a3, a4, slabs, out, held):
    capacity = a0.shape[0]
    for o, part in enumerate((a0, a1, a2, a3, a4)):
        held[o * capacity : (o + 1) * capacity] = part[...]
    peers = slabs.shape[0]
    share = out.shape[0] // peers - 1

    def one(i, carry):
        for f in range(share):
            out[i * (share + 1) + f] = held[slot[i * share + f]]
        out[i * (share + 1) + share] = slabs[i]
        return carry

    lax.fori_loop(0, peers, one, 0)


def turn_kernel(place, vectors, scales, jacobian, out):
    peers = vectors.shape[0] // vectors.shape[1]
    share = jacobian.shape[0] // peers
    first = place[0] * share
    count = place[1]
    half = MEM
    same = iota2(half, half, 0) // 32 == iota2(half, half, 1) // 32
    turns = []
    for h in range(2):
        block = vectors[h * half : (h + 1) * half, :]
        wide = jnp.where(same, jnp.concatenate([block] * 8, axis=1), 0.0) * scales[h : h + 1, :]
        turns.append(split(wide.T))
    for f in range(share):
        live = jnp.where(first + f < count, 1.0, 0.0).astype(F32)
        for h in range(2):
            block = jnp.concatenate(
                [jacobian[(h * 8 + s) * share + f] for s in range(8)], axis=0
            )
            high, low = turns[h]
            turned = (nn(high, block) + nn(low, block)) * live
            out[f, h * half : (h + 1) * half, :] = turned.astype(BF16)


def terms_kernel(place, turned, arrived, keep, give):
    share = turned.shape[0]
    peers = arrived.shape[0] // (share + 1)
    first = place[0] * share
    count = place[1]
    b = arrived[share].astype(F32)
    for source in range(1, peers):
        b = b + arrived[source * (share + 1) + share].astype(F32)
    gram = jnp.zeros((MEM, MEM), F32)
    pull = jnp.zeros((8, MEM), F32)
    for f in range(share):
        live = jnp.where(first + f < count, 1.0, 0.0).astype(F32)
        column = jnp.concatenate(
            [arrived[s * (share + 1) + f] for s in range(peers)], axis=0
        )
        flipped = column.astype(F32).T.astype(BF16)
        whitened = nt(flipped, turned[f]).astype(BF16)
        gram = gram + nt(whitened, whitened)
        mine = iota2(8, 128, 0) == f % 8
        high, low = split(jnp.where(mine, b[:, 128 * (f // 8) : 128 * (f // 8) + 128] * live, 0.0))
        pull = pull + (nn(high, column) + nn(low, column))
    total = jnp.sum(pull, axis=0, keepdims=True)
    last = jnp.concatenate(
        [total[:, 0:128], total[:, 128:256], jnp.zeros((6, 128), F32)], axis=0
    )
    halves = (
        (gram[0:128, 0:128], gram[128:192, 0:128], last),
        (gram[128:256, 128:256], gram[192:256, 0:128], jnp.zeros_like(last)),
    )
    even = lax.rem(place[0], 2) == 0
    for out, (first_half, second_half) in ((keep, halves), (give, halves[::-1])):
        x, y, z = (jnp.where(even, p, q) for p, q in zip(first_half, second_half))
        out[0:16] = x.reshape(16, 8, 128)
        out[16:24] = y.reshape(8, 8, 128)
        out[24] = z
        out[25:32] = jnp.zeros((7, 8, 128), F32)


def lower_half(x):
    i, j = iota2(MEM, MEM, 0), iota2(MEM, MEM, 1)
    return jnp.where(i > j, x, jnp.where(i == j, 0.5 * x, 0.0))


def solve_kernel(
    place, mine, other, basis, ensemble, out, system, inverse, rows, held, sems
):
    eye = (iota2(MEM, MEM, 0) == iota2(MEM, MEM, 1)).astype(F32)
    even = lax.rem(place[0], 2) == 0
    low = jnp.where(even, mine[...], other[...])
    high = jnp.where(even, other[...], mine[...])
    g00 = low[0:16].reshape(128, 128)
    g11 = high[0:16].reshape(128, 128)
    g10 = jnp.concatenate(
        [low[16:24].reshape(64, 128), high[16:24].reshape(64, 128)], axis=0
    )
    last = low[24]
    pull = jnp.concatenate([last[0:1, :], last[1:2, :]], axis=1)
    a = jnp.concatenate(
        [jnp.concatenate([g00, g10.T], axis=1), jnp.concatenate([g10, g11], axis=1)], axis=0
    ) + (MEM - 1.0) * eye
    system[...] = a
    across = lax.rsqrt(jnp.sum(a * eye, axis=0, keepdims=True))
    down = lax.rsqrt(jnp.sum(a * eye, axis=1, keepdims=True))
    x = across * (eye - lower_half(a * across * down - eye))
    residual = nt(nn(x, a), x) - eye
    inverse[...] = x - nn(lower_half(residual), x)

    def go_on(state):
        step, size = state
        return jnp.logical_and(step < 9, jnp.logical_and(size >= 1e-4, size < 1e6))

    def refine(state):
        step, _ = state
        x = inverse[...]
        residual = nt(nn(x, system[...], HI), x, HI) - eye
        inverse[...] = x - nn(lower_half(residual), x)
        return step + 1, jnp.sum(residual * residual)

    _, size = lax.while_loop(go_on, refine, (jnp.int32(0), jnp.float32(1.0)))

    @pl.when(jnp.logical_not(size < 1e-4))
    def _():
        rows[:, 0:MEM] = system[...]
        rows[:, MEM : 2 * MEM] = eye
        lanes = iota2(1, 2 * MEM, 1)

        def eliminate(j, carry):
            row = rows[pl.ds(j, 1), :]
            pivot = jnp.sum(jnp.where(lanes == j, row, 0.0), axis=1, keepdims=True)
            old = rows[...]
            column = jnp.sum(jnp.where(lanes == j, old, 0.0), axis=1, keepdims=True)
            below = iota2(MEM, 1, 0) > j
            rows[...] = old - jnp.where(below, column / pivot, 0.0) * row
            rows[pl.ds(j, 1), :] = row * (1.0 / jnp.sqrt(pivot))
            return carry

        lax.fori_loop(0, MEM, eliminate, 0)
        inverse[...] = rows[:, MEM : 2 * MEM]

    x = inverse[...]
    halfway = jnp.sum(x * pull, axis=1, keepdims=True)
    target = (MEM - 1.0) ** 0.5 * basis[...] + halfway
    transform = nn(x.T, target, HI).astype(BF16)
    copies = []
    for i in range(held.shape[0]):
        size = held.shape[1]
        held[i] = nn(ensemble[i * size : (i + 1) * size, :], transform).astype(BF16)
        copies.append(
            pltpu.make_async_copy(held.at[i], out.at[i * size : (i + 1) * size], sems.at[i])
        )
        copies[-1].start()
    for copy in copies:
        copy.wait()


def send_by(value, axis, steps):
    count = lax.axis_size(axis)
    return lax.ppermute(value, axis, [(s, (s + steps) % count) for s in range(count)])


def swap(x, axis):
    return lax.all_to_all(x, axis, 0, 0, tiled=True)


def other_core(x):
    return lax.ppermute(x, CORE, [(0, 1), (1, 0)])


def summed_everywhere(keep, give):
    tiles = keep + other_core(give)
    mine = jnp.sum(swap(tiles, NEAR), axis=0, keepdims=True)
    far = lax.axis_size(FAR)
    mine = jnp.sum(swap(jnp.broadcast_to(mine, (far, 8, 128)), FAR), axis=0, keepdims=True)
    mine = swap(jnp.broadcast_to(mine, tiles.shape), NEAR)
    return mine, other_core(mine)


def local(
    ensemble,
    jacobian,
    innovation,
    error_vectors,
    error_values,
    ensemble_vectors,
    column_pick,
    footprint_slot,
    footprint_count,
):
    window, capacity = column_pick.shape[1:]
    levels, members = ensemble.shape[1:]
    width = error_vectors.shape[1]
    foot_rows = jacobian.shape[0]
    peers = lax.axis_size(CHAN)
    share = foot_rows // peers
    slab = (levels, members)

    sensitivity = swap(jacobian, CHAN)

    chosen = pl.pallas_call(
        pick_kernel,
        out_shape=[jax.ShapeDtypeStruct((capacity, *slab), BF16)] * window,
        in_specs=[SM, VM],
        out_specs=[VM] * window,
        compiler_params=PARAMS,
        cost_estimate=cost(0, 2 * ensemble.size),
        name="pick",
    )(column_pick.reshape(-1), ensemble)
    parts = []
    for o in range(window):
        steps = o - window // 2
        parts.append(send_by(chosen[o], TILE, steps) if steps else chosen[o])

    place = jnp.concatenate(
        [lax.axis_index(CHAN).astype(jnp.int32)[None], footprint_count.astype(jnp.int32)]
    )
    slabs = pl.pallas_call(
        weights_kernel,
        out_shape=jax.ShapeDtypeStruct((peers, *slab), BF16),
        in_specs=[SM, VM, VM, VM, VM],
        out_specs=VM,
        scratch_shapes=[pltpu.VMEM((foot_rows, 128), F32)],
        compiler_params=PARAMS,
        cost_estimate=cost(2 * foot_rows * 256 * 128, 2 * jacobian.size),
        name="weights",
    )(place, innovation, error_vectors, 1.0 / error_values.reshape(peers, width), jacobian)

    payload = pl.pallas_call(
        slot_kernel,
        out_shape=jax.ShapeDtypeStruct((foot_rows + peers, *slab), BF16),
        in_specs=[SM] + [VM] * (window + 1),
        out_specs=VM,
        scratch_shapes=[pltpu.VMEM((window * capacity, *slab), BF16)],
        compiler_params=PARAMS,
        cost_estimate=cost(0, 4 * foot_rows * levels * members),
        name="slots",
    )(footprint_slot, *parts, slabs)
    payload, sensitivity = lax.optimization_barrier((payload, sensitivity))
    arrived = swap(payload, CHAN)

    turned = pl.pallas_call(
        turn_kernel,
        out_shape=jax.ShapeDtypeStruct((share, peers * width, 128), BF16),
        in_specs=[SM, VM, VM, VM],
        out_specs=VM,
        compiler_params=PARAMS,
        cost_estimate=cost(4 * 512 * share * 256 * 128, 4 * jacobian.size),
        name="turn",
    )(place, error_vectors, 1.0 / jnp.sqrt(error_values).reshape(2, members), sensitivity)

    keep, give = pl.pallas_call(
        terms_kernel,
        out_shape=[jax.ShapeDtypeStruct((32, 8, 128), F32)] * 2,
        in_specs=[SM, VM, VM],
        out_specs=[VM, VM],
        compiler_params=PARAMS,
        cost_estimate=cost(2 * 512 * share * 256 * 384, 2 * jacobian.size),
        name="terms",
    )(place, turned, arrived)

    mine, other = summed_everywhere(keep, give)

    chunks = 6
    flat_rows = ensemble.reshape(-1, members)
    updated = pl.pallas_call(
        solve_kernel,
        out_shape=jax.ShapeDtypeStruct(flat_rows.shape, BF16),
        in_specs=[SM, VM, VM, VM, VM],
        out_specs=pl.BlockSpec(memory_space=pl.ANY),
        scratch_shapes=[
            pltpu.VMEM((members, members), F32),
            pltpu.VMEM((members, members), F32),
            pltpu.VMEM((members, 2 * members), F32),
            pltpu.VMEM((chunks, flat_rows.shape[0] // chunks, members), BF16),
            pltpu.SemaphoreType.DMA((chunks,)),
        ],
        compiler_params=PARAMS,
        name="solve",
    )(place, mine, other, ensemble_vectors, flat_rows)
    return updated.reshape(ensemble.shape)


def solution(mesh):
    finer = Mesh(mesh.devices.reshape(8, 4, 8, 2), ("y", "x", "z", "c"))
    return jax.shard_map(
        local,
        mesh=finer,
        in_specs=(
            P(TILE, CHAN, None),
            P(TILE, CHAN, None),
            P(TILE, CHAN),
            P(),
            P(),
            P(),
            P(TILE, None, None),
            P(TILE),
            P(TILE),
        ),
        out_specs=P(TILE, CHAN, None),
        check_vma=False,
    )
```

```python
import jax
import jax.numpy as jnp
from jax import lax
from jax.experimental import pallas as pl
from jax.experimental.pallas import tpu as pltpu
from jax.sharding import Mesh
from jax.sharding import PartitionSpec as P

TILE = ("y", "x")
CHAN = ("z", "c")
NEAR = ("x", "z", "c")
FAR = "y"
MEM = 256
HI = lax.Precision.HIGHEST
F32 = jnp.float32
BF16 = jnp.bfloat16
VM = pl.BlockSpec(memory_space=pltpu.VMEM)
SM = pl.BlockSpec(memory_space=pltpu.SMEM)
PARAMS = pltpu.CompilerParams(vmem_limit_bytes=20 * 2**20)


def cost(flops, size):
    return pl.CostEstimate(flops=flops, bytes_accessed=size, transcendentals=0)


def iota2(rows, columns, dim):
    return lax.broadcasted_iota(jnp.int32, (rows, columns), dim)


def nt(a, b, precision=None):
    return lax.dot_general(
        a, b, (((1,), (1,)), ((), ())), precision=precision, preferred_element_type=F32
    )


def nn(a, b, precision=None):
    return lax.dot_general(
        a, b, (((1,), (0,)), ((), ())), precision=precision, preferred_element_type=F32
    )


def split(x):
    high = x.astype(BF16)
    return high, (x - high.astype(F32)).astype(BF16)


def pick_kernel(pick, ensemble, *sends):
    capacity = sends[0].shape[0]
    for o, out in enumerate(sends):

        def one(j, carry, o=o, out=out):
            out[j] = ensemble[pick[o * capacity + j]]
            return carry

        lax.fori_loop(0, capacity, one, 0, unroll=8)


def misfit_kernel(place, innovation, vectors, scales, out):
    group = place[0]
    width = vectors.shape[1]
    start = pl.multiple_of(group * width, width)
    basis = vectors[pl.ds(start, width), :] * scales[pl.ds(group, 1), :]
    misfit = nn(innovation[...], basis, HI)
    peers = out.shape[0]
    share = misfit.shape[0] // peers
    rest = jnp.zeros((16 - share, width), F32)
    blank = jnp.zeros((8, 128 - 2 * width), F32)
    for i in range(peers):
        left = misfit[share * i : share * i + 8, :]
        right = jnp.concatenate([misfit[share * i + 8 : share * (i + 1), :], rest], axis=0)
        out[i] = jnp.concatenate([left, right, blank], axis=1).astype(BF16)


def slot_kernel(slot, a0, a1, a2, a3, a4, misfits, out, held):
    capacity = a0.shape[0]
    for o, part in enumerate((a0, a1, a2, a3, a4)):
        held[o * capacity : (o + 1) * capacity] = part[...]
    peers = misfits.shape[0]
    step = out.shape[0] // peers
    share = step // 2

    def one(i, carry):
        for f in range(share):
            column = held[slot[i * share + f]]
            out[i * step + 2 * f] = column[:, 0:128]
            out[i * step + 2 * f + 1] = column[:, 128:256]
        out[i * step + 2 * share] = misfits[i]
        return carry

    lax.fori_loop(0, peers, one, 0)


def turn_kernel(place, vectors, scales, jacobian, out):
    peers = vectors.shape[0] // vectors.shape[1]
    share = jacobian.shape[0] // peers
    first = place[0] * share
    count = place[1]
    half = MEM
    same = iota2(half, half, 0) // 32 == iota2(half, half, 1) // 32
    turns = []
    for h in range(2):
        block = vectors[h * half : (h + 1) * half, :]
        wide = jnp.where(same, jnp.concatenate([block] * 8, axis=1), 0.0) * scales[h : h + 1, :]
        turns.append(split(wide.T))
    for f in range(share):
        live = jnp.where(first + f < count, 1.0, 0.0).astype(F32)
        for h in range(2):
            block = jnp.concatenate(
                [jacobian[(h * 8 + s) * share + f] for s in range(8)], axis=0
            )
            high, low = turns[h]
            turned = (nn(high, block) + nn(low, block)) * live
            out[f, h * half : (h + 1) * half, :] = turned.astype(BF16)


def terms_kernel(turned, arrived, out):
    share, channels = turned.shape[:2]
    step = 2 * share + 1
    peers = arrived.shape[0] // step
    width = channels // peers
    tiles = [arrived[s * step + 2 * share].astype(F32) for s in range(peers)]
    misfit = [
        jnp.concatenate([t[:, width * k : width * (k + 1)] for t in tiles], axis=1)
        for k in range(2)
    ]
    blank = jnp.zeros((8, channels), F32)
    gram = jnp.zeros((MEM + 16, MEM), F32)
    batch = 5
    for begin in range(0, share, batch):
        lefts, rights = [], []
        for f in range(begin, begin + batch):
            flipped = []
            for h in range(2):
                column = jnp.concatenate(
                    [arrived[s * step + 2 * f + h] for s in range(peers)], axis=0
                )
                flipped.append(column.astype(F32).T.astype(BF16))
            whitened = nt(jnp.concatenate(flipped, axis=0), turned[f]).astype(BF16)
            row = jnp.where(iota2(8, channels, 0) == f % 8, misfit[f // 8], 0.0)
            rows = jnp.concatenate([row, blank], axis=0).astype(BF16)
            rights.append(whitened)
            lefts.append(jnp.concatenate([whitened, rows], axis=0))
        gram = gram + nt(jnp.concatenate(lefts, axis=1), jnp.concatenate(rights, axis=1))
    pull = gram[MEM : MEM + 16, :]
    out[0:16] = gram[0:128, 0:128].reshape(16, 8, 128)
    out[16:32] = gram[128:256, 0:128].reshape(16, 8, 128)
    out[32:48] = gram[128:256, 128:256].reshape(16, 8, 128)
    total = jnp.sum(pull, axis=0, keepdims=True)
    last = jnp.concatenate(
        [total[:, 0:128], total[:, 128:256], jnp.zeros((6, 128), F32)], axis=0
    )
    out[48:64] = jnp.zeros((16, 8, 128), F32)
    out[48] = last


def lower_half(x):
    i, j = iota2(MEM, MEM, 0), iota2(MEM, MEM, 1)
    return jnp.where(i > j, x, jnp.where(i == j, 0.5 * x, 0.0))


def nn3(a, b):
    (ah, al), (bh, bl) = split(a), split(b)
    return nn(ah, bh) + (nn(ah, bl) + nn(al, bh))


def nt3(a, b):
    (ah, al), (bh, bl) = split(a), split(b)
    return nt(ah, bh) + (nt(ah, bl) + nt(al, bh))


def corrected(x, residual):
    return x - nn(lower_half(residual).astype(BF16), x.astype(BF16))


def solve_kernel(summed, basis, ensemble, out, system, inverse, rows, held, sems):
    eye = (iota2(MEM, MEM, 0) == iota2(MEM, MEM, 1)).astype(F32)
    g00 = summed[0:16].reshape(128, 128)
    g10 = summed[16:32].reshape(128, 128)
    g11 = summed[32:48].reshape(128, 128)
    a = jnp.concatenate(
        [jnp.concatenate([g00, g10.T], axis=1), jnp.concatenate([g10, g11], axis=1)], axis=0
    ) + (MEM - 1.0) * eye
    system[...] = a
    across = lax.rsqrt(jnp.sum(a * eye, axis=0, keepdims=True))
    down = lax.rsqrt(jnp.sum(a * eye, axis=1, keepdims=True))
    x = across * (eye - lower_half(a * across * down - eye))
    rough = x.astype(BF16)
    x = corrected(x, nt(nn(rough, a.astype(BF16)).astype(BF16), rough) - eye)
    inverse[...] = corrected(x, nt3(nn3(x, a), x) - eye)

    def go_on(state):
        step, size = state
        return jnp.logical_and(step < 9, jnp.logical_and(size >= 1e-4, size < 1e6))

    def refine(state):
        step, _ = state
        x = inverse[...]
        residual = nt(nn(x, system[...], HI), x, HI) - eye
        inverse[...] = corrected(x, residual)
        return step + 1, jnp.sum(residual * residual)

    _, size = lax.while_loop(go_on, refine, (jnp.int32(0), jnp.float32(1.0)))

    @pl.when(jnp.logical_not(size < 1e-4))
    def _():
        rows[:, 0:MEM] = system[...]
        rows[:, MEM : 2 * MEM] = eye
        lanes = iota2(1, 2 * MEM, 1)

        def eliminate(j, carry):
            row = rows[pl.ds(j, 1), :]
            pivot = jnp.sum(jnp.where(lanes == j, row, 0.0), axis=1, keepdims=True)
            old = rows[...]
            column = jnp.sum(jnp.where(lanes == j, old, 0.0), axis=1, keepdims=True)
            below = iota2(MEM, 1, 0) > j
            rows[...] = old - jnp.where(below, column / pivot, 0.0) * row
            rows[pl.ds(j, 1), :] = row * (1.0 / jnp.sqrt(pivot))
            return carry

        lax.fori_loop(0, MEM, eliminate, 0)
        inverse[...] = rows[:, MEM : 2 * MEM]

    x = inverse[...]
    last = summed[48]
    pull = jnp.concatenate([last[0:1, :], last[1:2, :]], axis=1)
    halfway = jnp.sum(x * pull, axis=1, keepdims=True)
    target = (MEM - 1.0) ** 0.5 * basis[...] + halfway
    transform = nn3(x.T, target).astype(BF16)
    copies = []
    for i in range(held.shape[0]):
        size = held.shape[1]
        held[i] = nn(ensemble[i * size : (i + 1) * size, :], transform).astype(BF16)
        copies.append(
            pltpu.make_async_copy(held.at[i], out.at[i * size : (i + 1) * size], sems.at[i])
        )
        copies[-1].start()
    for copy in copies:
        copy.wait()


def send_by(value, axis, steps):
    count = lax.axis_size(axis)
    return lax.ppermute(value, axis, [(s, (s + steps) % count) for s in range(count)])


def swap(x, axis):
    return lax.all_to_all(x, axis, 0, 0, tiled=True)


def summed_everywhere(tiles):
    mine = jnp.sum(swap(tiles, NEAR), axis=0, keepdims=True)
    far = lax.axis_size(FAR)
    mine = jnp.sum(swap(jnp.broadcast_to(mine, (far, 8, 128)), FAR), axis=0, keepdims=True)
    return swap(jnp.broadcast_to(mine, (tiles.shape[0], 8, 128)), NEAR)


def local(
    ensemble,
    jacobian,
    innovation,
    error_vectors,
    error_values,
    ensemble_vectors,
    column_pick,
    footprint_slot,
    footprint_count,
):
    window, capacity = column_pick.shape[1:]
    levels, members = ensemble.shape[1:]
    width = error_vectors.shape[1]
    foot_rows = jacobian.shape[0]
    peers = lax.axis_size(CHAN)
    share = foot_rows // peers
    slab = (levels, members)

    sensitivity = swap(jacobian, CHAN)

    chosen = pl.pallas_call(
        pick_kernel,
        out_shape=[jax.ShapeDtypeStruct((capacity, *slab), BF16)] * window,
        in_specs=[SM, VM],
        out_specs=[VM] * window,
        compiler_params=PARAMS,
        cost_estimate=cost(0, 2 * ensemble.size),
        name="pick",
    )(column_pick.reshape(-1), ensemble)
    parts = []
    for o in range(window):
        steps = o - window // 2
        parts.append(send_by(chosen[o], TILE, steps) if steps else chosen[o])

    place = jnp.concatenate(
        [lax.axis_index(CHAN).astype(jnp.int32)[None], footprint_count.astype(jnp.int32)]
    )
    scales = 1.0 / jnp.sqrt(error_values)
    misfits = pl.pallas_call(
        misfit_kernel,
        out_shape=jax.ShapeDtypeStruct((peers, 8, 128), BF16),
        in_specs=[SM, VM, VM, VM],
        out_specs=VM,
        compiler_params=PARAMS,
        cost_estimate=cost(2 * foot_rows * width * width, 4 * error_vectors.size),
        name="misfit",
    )(place, innovation, error_vectors, scales.reshape(peers, width))

    payload = pl.pallas_call(
        slot_kernel,
        out_shape=jax.ShapeDtypeStruct((2 * foot_rows + peers, 8, 128), BF16),
        in_specs=[SM] + [VM] * (window + 1),
        out_specs=VM,
        scratch_shapes=[pltpu.VMEM((window * capacity, *slab), BF16)],
        compiler_params=PARAMS,
        cost_estimate=cost(0, 4 * foot_rows * levels * members),
        name="slots",
    )(footprint_slot, *parts, misfits)
    payload, sensitivity = lax.optimization_barrier((payload, sensitivity))
    arrived = swap(payload, CHAN)

    turned = pl.pallas_call(
        turn_kernel,
        out_shape=jax.ShapeDtypeStruct((share, peers * width, 128), BF16),
        in_specs=[SM, VM, VM, VM],
        out_specs=VM,
        compiler_params=PARAMS,
        cost_estimate=cost(4 * 512 * share * 256 * 128, 4 * jacobian.size),
        name="turn",
    )(place, error_vectors, scales.reshape(2, members), sensitivity)

    tiles = pl.pallas_call(
        terms_kernel,
        out_shape=jax.ShapeDtypeStruct((64, 8, 128), F32),
        in_specs=[VM, VM],
        out_specs=VM,
        compiler_params=PARAMS,
        cost_estimate=cost(2 * 512 * share * 256 * 384, 2 * jacobian.size),
        name="terms",
    )(turned, arrived)

    summed = summed_everywhere(tiles)

    chunks = 6
    flat_rows = ensemble.reshape(-1, members)
    updated = pl.pallas_call(
        solve_kernel,
        out_shape=jax.ShapeDtypeStruct(flat_rows.shape, BF16),
        in_specs=[VM, VM, VM],
        out_specs=pl.BlockSpec(memory_space=pl.ANY),
        scratch_shapes=[
            pltpu.VMEM((members, members), F32),
            pltpu.VMEM((members, members), F32),
            pltpu.VMEM((members, 2 * members), F32),
            pltpu.VMEM((chunks, flat_rows.shape[0] // chunks, members), BF16),
            pltpu.SemaphoreType.DMA((chunks,)),
        ],
        compiler_params=PARAMS,
        name="solve",
    )(summed, ensemble_vectors, flat_rows)
    return updated.reshape(ensemble.shape)


def solution(mesh):
    finer = Mesh(mesh.devices.reshape(8, 4, 8, 2), ("y", "x", "z", "c"))
    return jax.shard_map(
        local,
        mesh=finer,
        in_specs=(
            P(TILE, CHAN, None),
            P(TILE, CHAN, None),
            P(TILE, CHAN),
            P(),
            P(),
            P(),
            P(TILE, None, None),
            P(TILE),
            P(TILE),
        ),
        out_specs=P(TILE, CHAN, None),
        check_vma=False,
    )
```

```python
import jax
import jax.numpy as jnp
from jax import lax
from jax.experimental import pallas as pl
from jax.experimental.pallas import tpu as pltpu
from jax.sharding import Mesh
from jax.sharding import PartitionSpec as P

TILE = ("y", "x")
CHAN = ("z", "c")
NEAR = ("x", "z", "c")
FAR = "y"
MEM = 256
HI = lax.Precision.HIGHEST
F32 = jnp.float32
BF16 = jnp.bfloat16
VM = pl.BlockSpec(memory_space=pltpu.VMEM)
SM = pl.BlockSpec(memory_space=pltpu.SMEM)
HB = pl.BlockSpec(memory_space=pltpu.HBM)
BATCH = 5
PARAMS = pltpu.CompilerParams(vmem_limit_bytes=20 * 2**20)
WHOLE = pltpu.CompilerParams(vmem_limit_bytes=57 * 2**20)


def cost(flops, size):
    return pl.CostEstimate(flops=flops, bytes_accessed=size, transcendentals=0)


def iota2(rows, columns, dim):
    return lax.broadcasted_iota(jnp.int32, (rows, columns), dim)


def nt(a, b, precision=None):
    return lax.dot_general(
        a, b, (((1,), (1,)), ((), ())), precision=precision, preferred_element_type=F32
    )


def nn(a, b, precision=None):
    return lax.dot_general(
        a, b, (((1,), (0,)), ((), ())), precision=precision, preferred_element_type=F32
    )


def split(x):
    high = x.astype(BF16)
    return high, (x - high.astype(F32)).astype(BF16)


def pick_kernel(pick, ensemble, *sends):
    capacity = sends[0].shape[0]
    for o, out in enumerate(sends):

        def one(j, carry, o=o, out=out):
            out[j] = ensemble[pick[o * capacity + j]]
            return carry

        lax.fori_loop(0, capacity, one, 0, unroll=8)


def misfit_kernel(place, innovation, vectors, scales, out):
    group = place[0]
    width = vectors.shape[1]
    start = pl.multiple_of(group * width, width)
    basis = vectors[pl.ds(start, width), :] * scales[pl.ds(group, 1), :]
    misfit = nn(innovation[...], basis, HI)
    peers = out.shape[0]
    share = misfit.shape[0] // peers
    rest = jnp.zeros((16 - share, width), F32)
    blank = jnp.zeros((8, 128 - 2 * width), F32)
    for i in range(peers):
        left = misfit[share * i : share * i + 8, :]
        right = jnp.concatenate([misfit[share * i + 8 : share * (i + 1), :], rest], axis=0)
        out[i] = jnp.concatenate([left, right, blank], axis=1).astype(BF16)


def slot_kernel(slot, a0, a1, a2, a3, a4, misfits, out, held, built, sems):
    capacity = a0.shape[0]
    for o, part in enumerate((a0, a1, a2, a3, a4)):
        held[o * capacity : (o + 1) * capacity] = part[...]
    peers, step = out.shape[:2]
    share = step // 2

    def one(i, carry):
        for f in range(share):
            column = held[slot[i * share + f]]
            built[i, 2 * f] = column[:, 0:128]
            built[i, 2 * f + 1] = column[:, 128:256]
        built[i, 2 * share] = misfits[i]
        return carry

    copies = []
    half = peers // 2
    for k in range(2):
        lax.fori_loop(k * half, (k + 1) * half, one, 0)
        piece = pl.ds(k * half, half)
        copies.append(pltpu.make_async_copy(built.at[piece], out.at[piece], sems.at[k]))
        copies[-1].start()
    for copy in copies:
        copy.wait()


def turn_kernel(place, vectors, scales, jacobian, out, built, sems):
    peers = vectors.shape[0] // vectors.shape[1]
    share = jacobian.shape[0] // peers
    first = place[0] * share
    count = place[1]
    half = MEM
    same = iota2(half, half, 0) // 32 == iota2(half, half, 1) // 32
    turns = []
    for h in range(2):
        block = vectors[h * half : (h + 1) * half, :]
        wide = jnp.where(same, jnp.concatenate([block] * 8, axis=1), 0.0) * scales[h : h + 1, :]
        turns.append(split(wide.T))
    copies = []
    for f in range(share):
        live = jnp.where(first + f < count, 1.0, 0.0).astype(F32)
        for h in range(2):
            block = jnp.concatenate(
                [jacobian[(h * 8 + s) * share + f] for s in range(8)], axis=0
            )
            high, low = turns[h]
            turned = (nn(high, block) + nn(low, block)) * live
            built[f, h * half : (h + 1) * half, :] = turned.astype(BF16)
        if f % BATCH == BATCH - 1:
            piece = pl.ds(f + 1 - BATCH, BATCH)
            copies.append(
                pltpu.make_async_copy(built.at[piece], out.at[piece], sems.at[f // BATCH])
            )
            copies[-1].start()
    for copy in copies:
        copy.wait()


def terms_kernel(turned_far, arrived_far, out, turned, arrived, sems):
    share, channels = turned.shape[:2]
    peers = arrived.shape[0]
    width = channels // peers
    loads = []
    for k in range(share // BATCH):
        first = 2 * BATCH * k
        count = 2 * BATCH if k < share // BATCH - 1 else 2 * BATCH + 1
        tiles = pl.ds(first, count)
        rows = pl.ds(BATCH * k, BATCH)
        pair = (
            pltpu.make_async_copy(arrived_far.at[:, tiles], arrived.at[:, tiles], sems.at[2 * k]),
            pltpu.make_async_copy(turned_far.at[rows], turned.at[rows], sems.at[2 * k + 1]),
        )
        for copy in pair:
            copy.start()
        loads.append(pair)
    batches = []
    for k in range(share // BATCH):
        loads[k][0].wait()
        columns = []
        for f in range(BATCH * k, BATCH * (k + 1)):
            flipped = []
            for h in range(2):
                column = jnp.concatenate([arrived[s, 2 * f + h] for s in range(peers)], axis=0)
                flipped.append(column.astype(F32).T.astype(BF16))
            columns.append(jnp.concatenate(flipped, axis=0))
        loads[k][1].wait()
        batches.append(
            [nt(column, turned[BATCH * k + i]).astype(BF16) for i, column in enumerate(columns)]
        )
    tiles = [arrived[s, 2 * share].astype(F32) for s in range(peers)]
    misfit = [
        jnp.concatenate([t[:, width * k : width * (k + 1)] for t in tiles], axis=1)
        for k in range(2)
    ]
    blank = jnp.zeros((8, channels), F32)
    gram = jnp.zeros((MEM + 16, MEM), F32)
    for k, batch in enumerate(batches):
        lefts = []
        for i, whitened in enumerate(batch):
            f = BATCH * k + i
            row = jnp.where(iota2(8, channels, 0) == f % 8, misfit[f // 8], 0.0)
            rows = jnp.concatenate([row, blank], axis=0).astype(BF16)
            lefts.append(jnp.concatenate([whitened, rows], axis=0))
        gram = gram + nt(jnp.concatenate(lefts, axis=1), jnp.concatenate(batch, axis=1))
    pull = gram[MEM : MEM + 16, :]
    out[0:16] = gram[0:128, 0:128].reshape(16, 8, 128)
    out[16:32] = gram[128:256, 0:128].reshape(16, 8, 128)
    out[32:48] = gram[128:256, 128:256].reshape(16, 8, 128)
    total = jnp.sum(pull, axis=0, keepdims=True)
    last = jnp.concatenate(
        [total[:, 0:128], total[:, 128:256], jnp.zeros((6, 128), F32)], axis=0
    )
    out[48:64] = jnp.zeros((16, 8, 128), F32)
    out[48] = last


def lower_half(x):
    i, j = iota2(MEM, MEM, 0), iota2(MEM, MEM, 1)
    return jnp.where(i > j, x, jnp.where(i == j, 0.5 * x, 0.0))


def nn3(a, b):
    (ah, al), (bh, bl) = split(a), split(b)
    return nn(ah, bh) + (nn(ah, bl) + nn(al, bh))


def nt3(a, b):
    (ah, al), (bh, bl) = split(a), split(b)
    return nt(ah, bh) + (nt(ah, bl) + nt(al, bh))


def corrected(x, residual):
    return x - nn(lower_half(residual).astype(BF16), x.astype(BF16))


def solve_kernel(summed, basis, ensemble, out, system, inverse, rows, held, sems):
    eye = (iota2(MEM, MEM, 0) == iota2(MEM, MEM, 1)).astype(F32)
    g00 = summed[0:16].reshape(128, 128)
    g10 = summed[16:32].reshape(128, 128)
    g11 = summed[32:48].reshape(128, 128)
    a = jnp.concatenate(
        [jnp.concatenate([g00, g10.T], axis=1), jnp.concatenate([g10, g11], axis=1)], axis=0
    ) + (MEM - 1.0) * eye
    system[...] = a
    across = lax.rsqrt(jnp.sum(a * eye, axis=0, keepdims=True))
    down = lax.rsqrt(jnp.sum(a * eye, axis=1, keepdims=True))
    x = across * (eye - lower_half(a * across * down - eye))
    rough = x.astype(BF16)
    x = corrected(x, nt(nn(rough, a.astype(BF16)).astype(BF16), rough) - eye)
    inverse[...] = corrected(x, nt3(nn3(x, a), x) - eye)

    def go_on(state):
        step, size = state
        return jnp.logical_and(step < 9, jnp.logical_and(size >= 1e-4, size < 1e6))

    def refine(state):
        step, _ = state
        x = inverse[...]
        residual = nt(nn(x, system[...], HI), x, HI) - eye
        inverse[...] = corrected(x, residual)
        return step + 1, jnp.sum(residual * residual)

    _, size = lax.while_loop(go_on, refine, (jnp.int32(0), jnp.float32(1.0)))

    @pl.when(jnp.logical_not(size < 1e-4))
    def _():
        rows[:, 0:MEM] = system[...]
        rows[:, MEM : 2 * MEM] = eye
        lanes = iota2(1, 2 * MEM, 1)

        def eliminate(j, carry):
            row = rows[pl.ds(j, 1), :]
            pivot = jnp.sum(jnp.where(lanes == j, row, 0.0), axis=1, keepdims=True)
            old = rows[...]
            column = jnp.sum(jnp.where(lanes == j, old, 0.0), axis=1, keepdims=True)
            below = iota2(MEM, 1, 0) > j
            rows[...] = old - jnp.where(below, column / pivot, 0.0) * row
            rows[pl.ds(j, 1), :] = row * (1.0 / jnp.sqrt(pivot))
            return carry

        lax.fori_loop(0, MEM, eliminate, 0)
        inverse[...] = rows[:, MEM : 2 * MEM]

    x = inverse[...]
    last = summed[48]
    pull = jnp.concatenate([last[0:1, :], last[1:2, :]], axis=1)
    halfway = jnp.sum(x * pull, axis=1, keepdims=True)
    target = (MEM - 1.0) ** 0.5 * basis[...] + halfway
    transform = nn3(x.T, target).astype(BF16)
    copies = []
    for i in range(held.shape[0]):
        size = held.shape[1]
        held[i] = nn(ensemble[i * size : (i + 1) * size, :], transform).astype(BF16)
        copies.append(
            pltpu.make_async_copy(held.at[i], out.at[i * size : (i + 1) * size], sems.at[i])
        )
        copies[-1].start()
    for copy in copies:
        copy.wait()


def send_by(value, axis, steps):
    count = lax.axis_size(axis)
    return lax.ppermute(value, axis, [(s, (s + steps) % count) for s in range(count)])


def swap(x, axis):
    return lax.all_to_all(x, axis, 0, 0, tiled=True)


def summed_everywhere(tiles):
    mine = jnp.sum(swap(tiles, NEAR), axis=0, keepdims=True)
    far = lax.axis_size(FAR)
    mine = jnp.sum(swap(jnp.broadcast_to(mine, (far, 8, 128)), FAR), axis=0, keepdims=True)
    return swap(jnp.broadcast_to(mine, (tiles.shape[0], 8, 128)), NEAR)


def local(
    ensemble,
    jacobian,
    innovation,
    error_vectors,
    error_values,
    ensemble_vectors,
    column_pick,
    footprint_slot,
    footprint_count,
):
    window, capacity = column_pick.shape[1:]
    levels, members = ensemble.shape[1:]
    width = error_vectors.shape[1]
    foot_rows = jacobian.shape[0]
    peers = lax.axis_size(CHAN)
    share = foot_rows // peers
    slab = (levels, members)

    sensitivity = swap(jacobian, CHAN)

    chosen = pl.pallas_call(
        pick_kernel,
        out_shape=[jax.ShapeDtypeStruct((capacity, *slab), BF16)] * window,
        in_specs=[SM, VM],
        out_specs=[VM] * window,
        compiler_params=PARAMS,
        cost_estimate=cost(0, 2 * ensemble.size),
        name="pick",
    )(column_pick.reshape(-1), ensemble)
    parts = []
    for o in range(window):
        steps = o - window // 2
        parts.append(send_by(chosen[o], TILE, steps) if steps else chosen[o])

    place = jnp.concatenate(
        [lax.axis_index(CHAN).astype(jnp.int32)[None], footprint_count.astype(jnp.int32)]
    )
    scales = 1.0 / jnp.sqrt(error_values)
    misfits = pl.pallas_call(
        misfit_kernel,
        out_shape=jax.ShapeDtypeStruct((peers, 8, 128), BF16),
        in_specs=[SM, VM, VM, VM],
        out_specs=VM,
        compiler_params=PARAMS,
        cost_estimate=cost(2 * foot_rows * width * width, 4 * error_vectors.size),
        name="misfit",
    )(place, innovation, error_vectors, scales.reshape(peers, width))

    payload = pl.pallas_call(
        slot_kernel,
        out_shape=jax.ShapeDtypeStruct((peers, 2 * share + 1, 8, 128), BF16),
        in_specs=[SM] + [VM] * (window + 1),
        out_specs=HB,
        scratch_shapes=[
            pltpu.VMEM((window * capacity, *slab), BF16),
            pltpu.VMEM((peers, 2 * share + 1, 8, 128), BF16),
            pltpu.SemaphoreType.DMA((2,)),
        ],
        compiler_params=WHOLE,
        cost_estimate=cost(0, 4 * foot_rows * levels * members),
        name="slots",
    )(footprint_slot, *parts, misfits)
    payload, sensitivity = lax.optimization_barrier((payload, sensitivity))
    arrived = swap(payload, CHAN)

    turned = pl.pallas_call(
        turn_kernel,
        out_shape=jax.ShapeDtypeStruct((share, peers * width, 128), BF16),
        in_specs=[SM, VM, VM, VM],
        out_specs=HB,
        scratch_shapes=[
            pltpu.VMEM((share, peers * width, 128), BF16),
            pltpu.SemaphoreType.DMA((share // BATCH,)),
        ],
        compiler_params=PARAMS,
        cost_estimate=cost(4 * 512 * share * 256 * 128, 4 * jacobian.size),
        name="turn",
    )(place, error_vectors, scales.reshape(2, members), sensitivity)

    tiles = pl.pallas_call(
        terms_kernel,
        out_shape=jax.ShapeDtypeStruct((64, 8, 128), F32),
        in_specs=[HB, HB],
        out_specs=VM,
        scratch_shapes=[
            pltpu.VMEM(turned.shape, BF16),
            pltpu.VMEM(arrived.shape, BF16),
            pltpu.SemaphoreType.DMA((2 * (share // BATCH),)),
        ],
        compiler_params=WHOLE,
        cost_estimate=cost(2 * 512 * share * 256 * 384, 2 * jacobian.size),
        name="terms",
    )(turned, arrived)

    summed = summed_everywhere(tiles)

    chunks = 6
    flat_rows = ensemble.reshape(-1, members)
    updated = pl.pallas_call(
        solve_kernel,
        out_shape=jax.ShapeDtypeStruct(flat_rows.shape, BF16),
        in_specs=[VM, VM, VM],
        out_specs=pl.BlockSpec(memory_space=pl.ANY),
        scratch_shapes=[
            pltpu.VMEM((members, members), F32),
            pltpu.VMEM((members, members), F32),
            pltpu.VMEM((members, 2 * members), F32),
            pltpu.VMEM((chunks, flat_rows.shape[0] // chunks, members), BF16),
            pltpu.SemaphoreType.DMA((chunks,)),
        ],
        compiler_params=PARAMS,
        name="solve",
    )(summed, ensemble_vectors, flat_rows)
    return updated.reshape(ensemble.shape)


def solution(mesh):
    finer = Mesh(mesh.devices.reshape(8, 4, 8, 2), ("y", "x", "z", "c"))
    return jax.shard_map(
        local,
        mesh=finer,
        in_specs=(
            P(TILE, CHAN, None),
            P(TILE, CHAN, None),
            P(TILE, CHAN),
            P(),
            P(),
            P(),
            P(TILE, None, None),
            P(TILE),
            P(TILE),
        ),
        out_specs=P(TILE, CHAN, None),
        check_vma=False,
    )
```

```python
import jax
import jax.numpy as jnp
from jax import lax
from jax.experimental import pallas as pl
from jax.experimental.pallas import tpu as pltpu
from jax.sharding import Mesh
from jax.sharding import PartitionSpec as P

TILE = ("y", "x")
CHAN = ("z", "c")
NEAR = ("x", "z", "c")
FAR = "y"
MEM = 256
HI = lax.Precision.HIGHEST
F32 = jnp.float32
BF16 = jnp.bfloat16
VM = pl.BlockSpec(memory_space=pltpu.VMEM)
SM = pl.BlockSpec(memory_space=pltpu.SMEM)


def grant(mebibytes):
    return pltpu.CompilerParams(vmem_limit_bytes=mebibytes * 2**20)


def cost(flops, size):
    return pl.CostEstimate(flops=flops, bytes_accessed=size, transcendentals=0)


def iota2(rows, columns, dim):
    return lax.broadcasted_iota(jnp.int32, (rows, columns), dim)


def nt(a, b, precision=None):
    return lax.dot_general(
        a, b, (((1,), (1,)), ((), ())), precision=precision, preferred_element_type=F32
    )


def nn(a, b, precision=None):
    return lax.dot_general(
        a, b, (((1,), (0,)), ((), ())), precision=precision, preferred_element_type=F32
    )


def split(x):
    high = x.astype(BF16)
    return high, (x - high.astype(F32)).astype(BF16)


def pick_kernel(pick, ensemble, *sends):
    capacity = sends[0].shape[0]
    for o, out in enumerate(sends):

        def one(j, carry, o=o, out=out):
            out[j] = ensemble[pick[o * capacity + j]]
            return carry

        lax.fori_loop(0, capacity, one, 0, unroll=8)


def misfit_kernel(place, innovation, vectors, scales, out):
    group = place[0]
    width = vectors.shape[1]
    start = pl.multiple_of(group * width, width)
    basis = vectors[pl.ds(start, width), :] * scales[pl.ds(group, 1), :]
    misfit = nn(innovation[...], basis, HI)
    peers = out.shape[0]
    share = misfit.shape[0] // peers
    rest = jnp.zeros((16 - share, width), F32)
    blank = jnp.zeros((8, 128 - 2 * width), F32)
    for i in range(peers):
        left = misfit[share * i : share * i + 8, :]
        right = jnp.concatenate([misfit[share * i + 8 : share * (i + 1), :], rest], axis=0)
        out[i] = jnp.concatenate([left, right, blank], axis=1).astype(BF16)


def slot_kernel(slot, a0, a1, a2, a3, a4, misfits, out, held):
    capacity = a0.shape[0]
    for o, part in enumerate((a0, a1, a2, a3, a4)):
        held[o * capacity : (o + 1) * capacity] = part[...]
    peers = misfits.shape[0]
    step = out.shape[0] // peers
    share = step // 2

    def one(i, carry):
        for f in range(share):
            column = held[slot[i * share + f]]
            out[i * step + 2 * f] = column[:, 0:128]
            out[i * step + 2 * f + 1] = column[:, 128:256]
        out[i * step + 2 * share] = misfits[i]
        return carry

    lax.fori_loop(0, peers, one, 0)


def turn_kernel(place, vectors, scales, jacobian, out):
    peers = vectors.shape[0] // vectors.shape[1]
    share = jacobian.shape[0] // peers
    first = place[0] * share
    count = place[1]
    half = MEM
    same = iota2(half, half, 0) // 32 == iota2(half, half, 1) // 32
    turns = []
    for h in range(2):
        block = vectors[h * half : (h + 1) * half, :]
        wide = jnp.where(same, jnp.concatenate([block] * 8, axis=1), 0.0) * scales[h : h + 1, :]
        turns.append(split(wide.T))
    for f in range(share):
        live = jnp.where(first + f < count, 1.0, 0.0).astype(F32)
        for h in range(2):
            block = jnp.concatenate(
                [jacobian[(h * 8 + s) * share + f] for s in range(8)], axis=0
            )
            high, low = turns[h]
            turned = (nn(high, block) + nn(low, block)) * live
            out[f, h * half : (h + 1) * half, :] = turned.astype(BF16)


def terms_kernel(turned, arrived, out):
    share, channels = turned.shape[:2]
    step = 2 * share + 1
    peers = arrived.shape[0] // step
    width = channels // peers
    tiles = [arrived[s * step + 2 * share].astype(F32) for s in range(peers)]
    misfit = [
        jnp.concatenate([t[:, width * k : width * (k + 1)] for t in tiles], axis=1)
        for k in range(2)
    ]
    blank = jnp.zeros((8, channels), F32)
    gram = jnp.zeros((MEM + 16, MEM), F32)
    batch = 5
    for begin in range(0, share, batch):
        lefts, rights = [], []
        for f in range(begin, begin + batch):
            flipped = []
            for h in range(2):
                column = jnp.concatenate(
                    [arrived[s * step + 2 * f + h] for s in range(peers)], axis=0
                )
                flipped.append(column.astype(F32).T.astype(BF16))
            whitened = nt(jnp.concatenate(flipped, axis=0), turned[f]).astype(BF16)
            row = jnp.where(iota2(8, channels, 0) == f % 8, misfit[f // 8], 0.0)
            rows = jnp.concatenate([row, blank], axis=0).astype(BF16)
            rights.append(whitened)
            lefts.append(jnp.concatenate([whitened, rows], axis=0))
        gram = gram + nt(jnp.concatenate(lefts, axis=1), jnp.concatenate(rights, axis=1))
    pull = gram[MEM : MEM + 16, :]
    out[0:16] = gram[0:128, 0:128].reshape(16, 8, 128)
    out[16:32] = gram[128:256, 0:128].reshape(16, 8, 128)
    out[32:48] = gram[128:256, 128:256].reshape(16, 8, 128)
    total = jnp.sum(pull, axis=0, keepdims=True)
    last = jnp.concatenate(
        [total[:, 0:128], total[:, 128:256], jnp.zeros((6, 128), F32)], axis=0
    )
    out[48:64] = jnp.zeros((16, 8, 128), F32)
    out[48] = last


def lower_half(x):
    i, j = iota2(MEM, MEM, 0), iota2(MEM, MEM, 1)
    return jnp.where(i > j, x, jnp.where(i == j, 0.5 * x, 0.0))


def nn3(a, b):
    (ah, al), (bh, bl) = split(a), split(b)
    return nn(ah, bh) + (nn(ah, bl) + nn(al, bh))


def nt3(a, b):
    (ah, al), (bh, bl) = split(a), split(b)
    return nt(ah, bh) + (nt(ah, bl) + nt(al, bh))


def corrected(x, residual):
    return x - nn(lower_half(residual).astype(BF16), x.astype(BF16))


def solve_kernel(summed, basis, ensemble, out, system, inverse, rows, held, sems):
    eye = (iota2(MEM, MEM, 0) == iota2(MEM, MEM, 1)).astype(F32)
    g00 = summed[0:16].reshape(128, 128)
    g10 = summed[16:32].reshape(128, 128)
    g11 = summed[32:48].reshape(128, 128)
    a = jnp.concatenate(
        [jnp.concatenate([g00, g10.T], axis=1), jnp.concatenate([g10, g11], axis=1)], axis=0
    ) + (MEM - 1.0) * eye
    system[...] = a
    across = lax.rsqrt(jnp.sum(a * eye, axis=0, keepdims=True))
    down = lax.rsqrt(jnp.sum(a * eye, axis=1, keepdims=True))
    x = across * (eye - lower_half(a * across * down - eye))
    rough = x.astype(BF16)
    x = corrected(x, nt(nn(rough, a.astype(BF16)).astype(BF16), rough) - eye)
    inverse[...] = corrected(x, nt3(nn3(x, a), x) - eye)

    def go_on(state):
        step, size = state
        return jnp.logical_and(step < 9, jnp.logical_and(size >= 1e-4, size < 1e6))

    def refine(state):
        step, _ = state
        x = inverse[...]
        residual = nt(nn(x, system[...], HI), x, HI) - eye
        inverse[...] = corrected(x, residual)
        return step + 1, jnp.sum(residual * residual)

    _, size = lax.while_loop(go_on, refine, (jnp.int32(0), jnp.float32(1.0)))

    @pl.when(jnp.logical_not(size < 1e-4))
    def _():
        rows[:, 0:MEM] = system[...]
        rows[:, MEM : 2 * MEM] = eye
        lanes = iota2(1, 2 * MEM, 1)

        def eliminate(j, carry):
            row = rows[pl.ds(j, 1), :]
            pivot = jnp.sum(jnp.where(lanes == j, row, 0.0), axis=1, keepdims=True)
            old = rows[...]
            column = jnp.sum(jnp.where(lanes == j, old, 0.0), axis=1, keepdims=True)
            below = iota2(MEM, 1, 0) > j
            rows[...] = old - jnp.where(below, column / pivot, 0.0) * row
            rows[pl.ds(j, 1), :] = row * (1.0 / jnp.sqrt(pivot))
            return carry

        lax.fori_loop(0, MEM, eliminate, 0)
        inverse[...] = rows[:, MEM : 2 * MEM]

    x = inverse[...]
    last = summed[48]
    pull = jnp.concatenate([last[0:1, :], last[1:2, :]], axis=1)
    halfway = jnp.sum(x * pull, axis=1, keepdims=True)
    target = (MEM - 1.0) ** 0.5 * basis[...] + halfway
    transform = nn3(x.T, target).astype(BF16)
    copies = []
    for i in range(held.shape[0]):
        size = held.shape[1]
        held[i] = nn(ensemble[i * size : (i + 1) * size, :], transform).astype(BF16)
        copies.append(
            pltpu.make_async_copy(held.at[i], out.at[i * size : (i + 1) * size], sems.at[i])
        )
        copies[-1].start()
    for copy in copies:
        copy.wait()


def send_by(value, axis, steps):
    count = lax.axis_size(axis)
    return lax.ppermute(value, axis, [(s, (s + steps) % count) for s in range(count)])


def swap(x, axis):
    return lax.all_to_all(x, axis, 0, 0, tiled=True)


def summed_everywhere(tiles):
    mine = jnp.sum(swap(tiles, NEAR), axis=0, keepdims=True)
    far = lax.axis_size(FAR)
    mine = jnp.sum(swap(jnp.broadcast_to(mine, (far, 8, 128)), FAR), axis=0, keepdims=True)
    return swap(jnp.broadcast_to(mine, (tiles.shape[0], 8, 128)), NEAR)


def local(
    ensemble,
    jacobian,
    innovation,
    error_vectors,
    error_values,
    ensemble_vectors,
    column_pick,
    footprint_slot,
    footprint_count,
):
    window, capacity = column_pick.shape[1:]
    levels, members = ensemble.shape[1:]
    width = error_vectors.shape[1]
    foot_rows = jacobian.shape[0]
    peers = lax.axis_size(CHAN)
    share = foot_rows // peers
    slab = (levels, members)

    sensitivity = swap(jacobian, CHAN)

    chosen = pl.pallas_call(
        pick_kernel,
        out_shape=[jax.ShapeDtypeStruct((capacity, *slab), BF16)] * window,
        in_specs=[SM, VM],
        out_specs=[VM] * window,
        compiler_params=grant(57),
        cost_estimate=cost(0, 2 * ensemble.size),
        name="pick",
    )(column_pick.reshape(-1), ensemble)
    parts = []
    for o in range(window):
        steps = o - window // 2
        parts.append(send_by(chosen[o], TILE, steps) if steps else chosen[o])

    place = jnp.concatenate(
        [lax.axis_index(CHAN).astype(jnp.int32)[None], footprint_count.astype(jnp.int32)]
    )
    scales = 1.0 / jnp.sqrt(error_values)
    misfits = pl.pallas_call(
        misfit_kernel,
        out_shape=jax.ShapeDtypeStruct((peers, 8, 128), BF16),
        in_specs=[SM, VM, VM, VM],
        out_specs=VM,
        compiler_params=grant(12),
        cost_estimate=cost(2 * foot_rows * width * width, 4 * error_vectors.size),
        name="misfit",
    )(place, innovation, error_vectors, scales.reshape(peers, width))

    payload = pl.pallas_call(
        slot_kernel,
        out_shape=jax.ShapeDtypeStruct((2 * foot_rows + peers, 8, 128), BF16),
        in_specs=[SM] + [VM] * (window + 1),
        out_specs=VM,
        scratch_shapes=[pltpu.VMEM((window * capacity, *slab), BF16)],
        compiler_params=grant(48),
        cost_estimate=cost(0, 4 * foot_rows * levels * members),
        name="slots",
    )(footprint_slot, *parts, misfits)
    payload, sensitivity = lax.optimization_barrier((payload, sensitivity))
    arrived = swap(payload, CHAN)

    turned = pl.pallas_call(
        turn_kernel,
        out_shape=jax.ShapeDtypeStruct((share, peers * width, 128), BF16),
        in_specs=[SM, VM, VM, VM],
        out_specs=VM,
        compiler_params=grant(6),
        cost_estimate=cost(4 * 512 * share * 256 * 128, 4 * jacobian.size),
        name="turn",
    )(place, error_vectors, scales.reshape(2, members), sensitivity)

    tiles = pl.pallas_call(
        terms_kernel,
        out_shape=jax.ShapeDtypeStruct((64, 8, 128), F32),
        in_specs=[VM, VM],
        out_specs=VM,
        compiler_params=grant(20),
        cost_estimate=cost(2 * 512 * share * 256 * 384, 2 * jacobian.size),
        name="terms",
    )(turned, arrived)

    summed = summed_everywhere(tiles)

    chunks = 6
    flat_rows = ensemble.reshape(-1, members)
    updated = pl.pallas_call(
        solve_kernel,
        out_shape=jax.ShapeDtypeStruct(flat_rows.shape, BF16),
        in_specs=[VM, VM, VM],
        out_specs=pl.BlockSpec(memory_space=pl.ANY),
        scratch_shapes=[
            pltpu.VMEM((members, members), F32),
            pltpu.VMEM((members, members), F32),
            pltpu.VMEM((members, 2 * members), F32),
            pltpu.VMEM((chunks, flat_rows.shape[0] // chunks, members), BF16),
            pltpu.SemaphoreType.DMA((chunks,)),
        ],
        compiler_params=grant(12),
        name="solve",
    )(summed, ensemble_vectors, flat_rows)
    return updated.reshape(ensemble.shape)


def solution(mesh):
    finer = Mesh(mesh.devices.reshape(8, 4, 8, 2), ("y", "x", "z", "c"))
    return jax.shard_map(
        local,
        mesh=finer,
        in_specs=(
            P(TILE, CHAN, None),
            P(TILE, CHAN, None),
            P(TILE, CHAN),
            P(),
            P(),
            P(),
            P(TILE, None, None),
            P(TILE),
            P(TILE),
        ),
        out_specs=P(TILE, CHAN, None),
        check_vma=False,
    )
```

```python
import jax
import jax.numpy as jnp
from jax import lax
from jax.experimental import pallas as pl
from jax.experimental.pallas import tpu as pltpu
from jax.sharding import Mesh
from jax.sharding import PartitionSpec as P

TILE = ("y", "x")
CHAN = ("z", "c")
NEAR = ("x", "z", "c")
FAR = "y"
MEM = 256
HI = lax.Precision.HIGHEST
F32 = jnp.float32
BF16 = jnp.bfloat16
VM = pl.BlockSpec(memory_space=pltpu.VMEM)
SM = pl.BlockSpec(memory_space=pltpu.SMEM)
ANY = pl.BlockSpec(memory_space=pl.ANY)


def grant(mebibytes):
    return pltpu.CompilerParams(vmem_limit_bytes=mebibytes * 2**20)


def cost(flops, size):
    return pl.CostEstimate(flops=flops, bytes_accessed=size, transcendentals=0)


def iota2(rows, columns, dim):
    return lax.broadcasted_iota(jnp.int32, (rows, columns), dim)


def nt(a, b, precision=None):
    return lax.dot_general(
        a, b, (((1,), (1,)), ((), ())), precision=precision, preferred_element_type=F32
    )


def nn(a, b, precision=None):
    return lax.dot_general(
        a, b, (((1,), (0,)), ((), ())), precision=precision, preferred_element_type=F32
    )


def split(x):
    high = x.astype(BF16)
    return high, (x - high.astype(F32)).astype(BF16)


def pick_kernel(pick, ensemble, *sends):
    capacity = sends[0].shape[0]
    for o, out in enumerate(sends):

        def one(j, carry, o=o, out=out):
            out[j] = ensemble[pick[o * capacity + j]]
            return carry

        lax.fori_loop(0, capacity, one, 0, unroll=8)


def misfit_kernel(place, innovation, vectors, scales, out):
    group = place[0]
    width = vectors.shape[1]
    start = pl.multiple_of(group * width, width)
    basis = vectors[pl.ds(start, width), :] * scales[pl.ds(group, 1), :]
    misfit = nn(innovation[...], basis, HI)
    peers = out.shape[0]
    share = misfit.shape[0] // peers
    rest = jnp.zeros((16 - share, width), F32)
    blank = jnp.zeros((8, 128 - 2 * width), F32)
    for i in range(peers):
        left = misfit[share * i : share * i + 8, :]
        right = jnp.concatenate([misfit[share * i + 8 : share * (i + 1), :], rest], axis=0)
        out[i] = jnp.concatenate([left, right, blank], axis=1).astype(BF16)


def slot_kernel(slot, a0, a1, a2, a3, a4, misfits, out, held):
    capacity = a0.shape[0]
    for o, part in enumerate((a0, a1, a2, a3, a4)):
        held[o * capacity : (o + 1) * capacity] = part[...]
    peers = misfits.shape[0]
    step = out.shape[0] // peers
    share = step // 2

    def one(i, carry):
        for f in range(share):
            column = held[slot[i * share + f]]
            out[i * step + 2 * f] = column[:, 0:128]
            out[i * step + 2 * f + 1] = column[:, 128:256]
        out[i * step + 2 * share] = misfits[i]
        return carry

    lax.fori_loop(0, peers, one, 0)


def turn_kernel(place, vectors, scales, jacobian, out):
    peers = vectors.shape[0] // vectors.shape[1]
    share = jacobian.shape[0] // peers
    first = place[0] * share
    count = place[1]
    half = MEM
    same = iota2(half, half, 0) // 32 == iota2(half, half, 1) // 32
    turns = []
    for h in range(2):
        block = vectors[h * half : (h + 1) * half, :]
        wide = jnp.where(same, jnp.concatenate([block] * 8, axis=1), 0.0) * scales[h : h + 1, :]
        turns.append(split(wide.T))
    for f in range(share):
        live = jnp.where(first + f < count, 1.0, 0.0).astype(F32)
        for h in range(2):
            block = jnp.concatenate(
                [jacobian[(h * 8 + s) * share + f] for s in range(8)], axis=0
            )
            high, low = turns[h]
            turned = (nn(high, block) + nn(low, block)) * live
            out[f, h * half : (h + 1) * half, :] = turned.astype(BF16)


def terms_kernel(turned, arrived, out):
    share, channels = turned.shape[:2]
    step = 2 * share + 1
    peers = arrived.shape[0] // step
    width = channels // peers
    tiles = [arrived[s * step + 2 * share].astype(F32) for s in range(peers)]
    misfit = [
        jnp.concatenate([t[:, width * k : width * (k + 1)] for t in tiles], axis=1)
        for k in range(2)
    ]
    blank = jnp.zeros((8, channels), F32)
    gram = jnp.zeros((MEM + 16, MEM), F32)
    batch = 5
    for begin in range(0, share, batch):
        lefts, rights = [], []
        for f in range(begin, begin + batch):
            flipped = []
            for h in range(2):
                column = jnp.concatenate(
                    [arrived[s * step + 2 * f + h] for s in range(peers)], axis=0
                )
                flipped.append(column.astype(F32).T.astype(BF16))
            whitened = nt(jnp.concatenate(flipped, axis=0), turned[f]).astype(BF16)
            row = jnp.where(iota2(8, channels, 0) == f % 8, misfit[f // 8], 0.0)
            rows = jnp.concatenate([row, blank], axis=0).astype(BF16)
            rights.append(whitened)
            lefts.append(jnp.concatenate([whitened, rows], axis=0))
        gram = gram + nt(jnp.concatenate(lefts, axis=1), jnp.concatenate(rights, axis=1))
    pull = gram[MEM : MEM + 16, :]
    out[0:16] = gram[0:128, 0:128].reshape(16, 8, 128)
    out[16:32] = gram[128:256, 0:128].reshape(16, 8, 128)
    out[32:48] = gram[128:256, 128:256].reshape(16, 8, 128)
    total = jnp.sum(pull, axis=0, keepdims=True)
    last = jnp.concatenate(
        [total[:, 0:128], total[:, 128:256], jnp.zeros((6, 128), F32)], axis=0
    )
    out[48:64] = jnp.zeros((16, 8, 128), F32)
    out[48] = last


def lower_half(x):
    i, j = iota2(MEM, MEM, 0), iota2(MEM, MEM, 1)
    return jnp.where(i > j, x, jnp.where(i == j, 0.5 * x, 0.0))


def nn3(a, b):
    (ah, al), (bh, bl) = split(a), split(b)
    return nn(ah, bh) + (nn(ah, bl) + nn(al, bh))


def nt3(a, b):
    (ah, al), (bh, bl) = split(a), split(b)
    return nt(ah, bh) + (nt(ah, bl) + nt(al, bh))


def corrected(x, residual):
    return x - nn(lower_half(residual).astype(BF16), x.astype(BF16))


def solve_kernel(
    summed, basis, ensemble_far, out, system, inverse, rows, ensemble, held, load_sem, sems
):
    load = pltpu.make_async_copy(ensemble_far, ensemble, load_sem)
    load.start()
    eye = (iota2(MEM, MEM, 0) == iota2(MEM, MEM, 1)).astype(F32)
    g00 = summed[0:16].reshape(128, 128)
    g10 = summed[16:32].reshape(128, 128)
    g11 = summed[32:48].reshape(128, 128)
    a = jnp.concatenate(
        [jnp.concatenate([g00, g10.T], axis=1), jnp.concatenate([g10, g11], axis=1)], axis=0
    ) + (MEM - 1.0) * eye
    system[...] = a
    across = lax.rsqrt(jnp.sum(a * eye, axis=0, keepdims=True))
    down = lax.rsqrt(jnp.sum(a * eye, axis=1, keepdims=True))
    x = across * (eye - lower_half(a * across * down - eye))
    rough = x.astype(BF16)
    x = corrected(x, nt(nn(rough, a.astype(BF16)).astype(BF16), rough) - eye)
    inverse[...] = corrected(x, nt3(nn3(x, a), x) - eye)

    def go_on(state):
        step, size = state
        return jnp.logical_and(step < 9, jnp.logical_and(size >= 1e-4, size < 1e6))

    def refine(state):
        step, _ = state
        x = inverse[...]
        residual = nt(nn(x, system[...], HI), x, HI) - eye
        inverse[...] = corrected(x, residual)
        return step + 1, jnp.sum(residual * residual)

    _, size = lax.while_loop(go_on, refine, (jnp.int32(0), jnp.float32(1.0)))

    @pl.when(jnp.logical_not(size < 1e-4))
    def _():
        rows[:, 0:MEM] = system[...]
        rows[:, MEM : 2 * MEM] = eye
        lanes = iota2(1, 2 * MEM, 1)

        def eliminate(j, carry):
            row = rows[pl.ds(j, 1), :]
            pivot = jnp.sum(jnp.where(lanes == j, row, 0.0), axis=1, keepdims=True)
            old = rows[...]
            column = jnp.sum(jnp.where(lanes == j, old, 0.0), axis=1, keepdims=True)
            below = iota2(MEM, 1, 0) > j
            rows[...] = old - jnp.where(below, column / pivot, 0.0) * row
            rows[pl.ds(j, 1), :] = row * (1.0 / jnp.sqrt(pivot))
            return carry

        lax.fori_loop(0, MEM, eliminate, 0)
        inverse[...] = rows[:, MEM : 2 * MEM]

    x = inverse[...]
    last = summed[48]
    pull = jnp.concatenate([last[0:1, :], last[1:2, :]], axis=1)
    halfway = jnp.sum(x * pull, axis=1, keepdims=True)
    target = (MEM - 1.0) ** 0.5 * basis[...] + halfway
    transform = nn3(x.T, target).astype(BF16)
    load.wait()
    copies = []
    for i in range(held.shape[0]):
        size = held.shape[1]
        held[i] = nn(ensemble[i * size : (i + 1) * size, :], transform).astype(BF16)
        copies.append(
            pltpu.make_async_copy(held.at[i], out.at[i * size : (i + 1) * size], sems.at[i])
        )
        copies[-1].start()
    for copy in copies:
        copy.wait()


def send_by(value, axis, steps):
    count = lax.axis_size(axis)
    return lax.ppermute(value, axis, [(s, (s + steps) % count) for s in range(count)])


def swap(x, axis):
    return lax.all_to_all(x, axis, 0, 0, tiled=True)


def summed_everywhere(tiles):
    mine = jnp.sum(swap(tiles, NEAR), axis=0, keepdims=True)
    far = lax.axis_size(FAR)
    mine = jnp.sum(swap(jnp.broadcast_to(mine, (far, 8, 128)), FAR), axis=0, keepdims=True)
    return swap(jnp.broadcast_to(mine, (tiles.shape[0], 8, 128)), NEAR)


def local(
    ensemble,
    jacobian,
    innovation,
    error_vectors,
    error_values,
    ensemble_vectors,
    column_pick,
    footprint_slot,
    footprint_count,
):
    window, capacity = column_pick.shape[1:]
    levels, members = ensemble.shape[1:]
    width = error_vectors.shape[1]
    foot_rows = jacobian.shape[0]
    peers = lax.axis_size(CHAN)
    share = foot_rows // peers
    slab = (levels, members)

    sensitivity = swap(jacobian, CHAN)

    chosen = pl.pallas_call(
        pick_kernel,
        out_shape=[jax.ShapeDtypeStruct((capacity, *slab), BF16)] * window,
        in_specs=[SM, VM],
        out_specs=[VM] * window,
        compiler_params=grant(20),
        cost_estimate=cost(0, 2 * ensemble.size),
        name="pick",
    )(column_pick.reshape(-1), ensemble)
    parts = []
    for o in range(window):
        steps = o - window // 2
        parts.append(send_by(chosen[o], TILE, steps) if steps else chosen[o])

    place = jnp.concatenate(
        [lax.axis_index(CHAN).astype(jnp.int32)[None], footprint_count.astype(jnp.int32)]
    )
    scales = 1.0 / jnp.sqrt(error_values)
    misfits = pl.pallas_call(
        misfit_kernel,
        out_shape=jax.ShapeDtypeStruct((peers, 8, 128), BF16),
        in_specs=[SM, VM, VM, VM],
        out_specs=VM,
        compiler_params=grant(20),
        cost_estimate=cost(2 * foot_rows * width * width, 4 * error_vectors.size),
        name="misfit",
    )(place, innovation, error_vectors, scales.reshape(peers, width))

    payload = pl.pallas_call(
        slot_kernel,
        out_shape=jax.ShapeDtypeStruct((2 * foot_rows + peers, 8, 128), BF16),
        in_specs=[SM] + [VM] * (window + 1),
        out_specs=VM,
        scratch_shapes=[pltpu.VMEM((window * capacity, *slab), BF16)],
        compiler_params=grant(20),
        cost_estimate=cost(0, 4 * foot_rows * levels * members),
        name="slots",
    )(footprint_slot, *parts, misfits)
    payload, sensitivity = lax.optimization_barrier((payload, sensitivity))
    arrived = swap(payload, CHAN)

    turned = pl.pallas_call(
        turn_kernel,
        out_shape=jax.ShapeDtypeStruct((share, peers * width, 128), BF16),
        in_specs=[SM, VM, VM, VM],
        out_specs=VM,
        compiler_params=grant(20),
        cost_estimate=cost(4 * 512 * share * 256 * 128, 4 * jacobian.size),
        name="turn",
    )(place, error_vectors, scales.reshape(2, members), sensitivity)

    tiles = pl.pallas_call(
        terms_kernel,
        out_shape=jax.ShapeDtypeStruct((64, 8, 128), F32),
        in_specs=[VM, VM],
        out_specs=VM,
        compiler_params=grant(20),
        cost_estimate=cost(2 * 512 * share * 256 * 384, 2 * jacobian.size),
        name="terms",
    )(turned, arrived)

    summed = summed_everywhere(tiles)

    chunks = 6
    flat_rows = ensemble.reshape(-1, members)
    updated = pl.pallas_call(
        solve_kernel,
        out_shape=jax.ShapeDtypeStruct(flat_rows.shape, BF16),
        in_specs=[VM, VM, ANY],
        out_specs=ANY,
        scratch_shapes=[
            pltpu.VMEM((members, members), F32),
            pltpu.VMEM((members, members), F32),
            pltpu.VMEM((members, 2 * members), F32),
            pltpu.VMEM(flat_rows.shape, BF16),
            pltpu.VMEM((chunks, flat_rows.shape[0] // chunks, members), BF16),
            pltpu.SemaphoreType.DMA,
            pltpu.SemaphoreType.DMA((chunks,)),
        ],
        compiler_params=grant(57),
        name="solve",
    )(summed, ensemble_vectors, flat_rows)
    return updated.reshape(ensemble.shape)


def solution(mesh):
    finer = Mesh(mesh.devices.reshape(8, 4, 8, 2), ("y", "x", "z", "c"))
    return jax.shard_map(
        local,
        mesh=finer,
        in_specs=(
            P(TILE, CHAN, None),
            P(TILE, CHAN, None),
            P(TILE, CHAN),
            P(),
            P(),
            P(),
            P(TILE, None, None),
            P(TILE),
            P(TILE),
        ),
        out_specs=P(TILE, CHAN, None),
        check_vma=False,
    )
```

```python
import jax
import jax.numpy as jnp
from jax import lax
from jax.experimental import pallas as pl
from jax.experimental.pallas import tpu as pltpu
from jax.sharding import Mesh
from jax.sharding import PartitionSpec as P

TILE = ("y", "x")
CHAN = ("z", "c")
NEAR = ("x", "z", "c")
FAR = "y"
MEM = 256
HI = lax.Precision.HIGHEST
F32 = jnp.float32
BF16 = jnp.bfloat16
VM = pl.BlockSpec(memory_space=pltpu.VMEM)
SM = pl.BlockSpec(memory_space=pltpu.SMEM)
ANY = pl.BlockSpec(memory_space=pl.ANY)


def grant(mebibytes):
    return pltpu.CompilerParams(vmem_limit_bytes=mebibytes * 2**20)


def cost(flops, size):
    return pl.CostEstimate(flops=flops, bytes_accessed=size, transcendentals=0)


def iota2(rows, columns, dim):
    return lax.broadcasted_iota(jnp.int32, (rows, columns), dim)


def nt(a, b, precision=None):
    return lax.dot_general(
        a, b, (((1,), (1,)), ((), ())), precision=precision, preferred_element_type=F32
    )


def nn(a, b, precision=None):
    return lax.dot_general(
        a, b, (((1,), (0,)), ((), ())), precision=precision, preferred_element_type=F32
    )


def split(x):
    high = x.astype(BF16)
    return high, (x - high.astype(F32)).astype(BF16)


def pick_kernel(pick, ensemble, *sends):
    capacity = sends[0].shape[0]
    for o, out in enumerate(sends):

        def one(j, carry, o=o, out=out):
            out[j] = ensemble[pick[o * capacity + j]]
            return carry

        lax.fori_loop(0, capacity, one, 0, unroll=8)


def misfit_kernel(place, innovation, vectors, scales, out):
    group = place[0]
    width = vectors.shape[1]
    start = pl.multiple_of(group * width, width)
    basis = vectors[pl.ds(start, width), :] * scales[pl.ds(group, 1), :]
    misfit = nn(innovation[...], basis, HI)
    peers = out.shape[0]
    share = misfit.shape[0] // peers
    rest = jnp.zeros((16 - share, width), F32)
    blank = jnp.zeros((8, 128 - 2 * width), F32)
    for i in range(peers):
        left = misfit[share * i : share * i + 8, :]
        right = jnp.concatenate([misfit[share * i + 8 : share * (i + 1), :], rest], axis=0)
        out[i] = jnp.concatenate([left, right, blank], axis=1).astype(BF16)


def slot_kernel(slot, a0, a1, a2, a3, a4, misfits, out, held):
    capacity = a0.shape[0]
    for o, part in enumerate((a0, a1, a2, a3, a4)):
        held[o * capacity : (o + 1) * capacity] = part[...]
    peers = misfits.shape[0]
    step = out.shape[0] // peers
    share = step // 2

    def one(i, carry):
        for f in range(share):
            column = held[slot[i * share + f]]
            out[i * step + 2 * f] = column[:, 0:128]
            out[i * step + 2 * f + 1] = column[:, 128:256]
        out[i * step + 2 * share] = misfits[i]
        return carry

    lax.fori_loop(0, peers, one, 0)


def turn_kernel(place, vectors, scales, jacobian, out):
    peers = vectors.shape[0] // vectors.shape[1]
    share = jacobian.shape[0] // peers
    first = place[0] * share
    count = place[1]
    half = MEM
    same = iota2(half, half, 0) // 32 == iota2(half, half, 1) // 32
    turns = []
    for h in range(2):
        block = vectors[h * half : (h + 1) * half, :]
        wide = jnp.where(same, jnp.concatenate([block] * 8, axis=1), 0.0) * scales[h : h + 1, :]
        turns.append(split(wide.T))
    for f in range(share):
        live = jnp.where(first + f < count, 1.0, 0.0).astype(F32)
        for h in range(2):
            block = jnp.concatenate(
                [jacobian[(h * 8 + s) * share + f] for s in range(8)], axis=0
            )
            high, low = turns[h]
            turned = (nn(high, block) + nn(low, block)) * live
            out[f, h * half : (h + 1) * half, :] = turned.astype(BF16)


def terms_kernel(turned, arrived, out):
    share, channels = turned.shape[:2]
    step = 2 * share + 1
    peers = arrived.shape[0] // step
    width = channels // peers
    tiles = [arrived[s * step + 2 * share].astype(F32) for s in range(peers)]
    misfit = [
        jnp.concatenate([t[:, width * k : width * (k + 1)] for t in tiles], axis=1)
        for k in range(2)
    ]
    blank = jnp.zeros((8, channels), F32)
    gram = jnp.zeros((MEM + 16, MEM), F32)
    batch = 5
    for begin in range(0, share, batch):
        lefts, rights = [], []
        for f in range(begin, begin + batch):
            flipped = []
            for h in range(2):
                column = jnp.concatenate(
                    [arrived[s * step + 2 * f + h] for s in range(peers)], axis=0
                )
                flipped.append(column.astype(F32).T.astype(BF16))
            whitened = nt(jnp.concatenate(flipped, axis=0), turned[f]).astype(BF16)
            row = jnp.where(iota2(8, channels, 0) == f % 8, misfit[f // 8], 0.0)
            rows = jnp.concatenate([row, blank], axis=0).astype(BF16)
            rights.append(whitened)
            lefts.append(jnp.concatenate([whitened, rows], axis=0))
        gram = gram + nt(jnp.concatenate(lefts, axis=1), jnp.concatenate(rights, axis=1))
    pull = gram[MEM : MEM + 16, :]
    out[0:16] = gram[0:128, 0:128].reshape(16, 8, 128)
    out[16:32] = gram[128:256, 0:128].reshape(16, 8, 128)
    out[32:48] = gram[128:256, 128:256].reshape(16, 8, 128)
    total = jnp.sum(pull, axis=0, keepdims=True)
    last = jnp.concatenate(
        [total[:, 0:128], total[:, 128:256], jnp.zeros((6, 128), F32)], axis=0
    )
    out[48:64] = jnp.zeros((16, 8, 128), F32)
    out[48] = last


def lower_half(x):
    i, j = iota2(MEM, MEM, 0), iota2(MEM, MEM, 1)
    return jnp.where(i > j, x, jnp.where(i == j, 0.5 * x, 0.0))


def nn3(a, b):
    (ah, al), (bh, bl) = split(a), split(b)
    return nn(ah, bh) + (nn(ah, bl) + nn(al, bh))


def nt3(a, b):
    (ah, al), (bh, bl) = split(a), split(b)
    return nt(ah, bh) + (nt(ah, bl) + nt(al, bh))


def corrected(x, residual):
    return x - nn(lower_half(residual).astype(BF16), x.astype(BF16))


def solve_kernel(
    summed, basis, ensemble_far, out, system, inverse, rows, ensemble, held, load_sem, sems
):
    load = pltpu.make_async_copy(ensemble_far, ensemble, load_sem)
    load.start()
    eye = (iota2(MEM, MEM, 0) == iota2(MEM, MEM, 1)).astype(F32)
    g00 = summed[0:16].reshape(128, 128)
    g10 = summed[16:32].reshape(128, 128)
    g11 = summed[32:48].reshape(128, 128)
    a = jnp.concatenate(
        [jnp.concatenate([g00, g10.T], axis=1), jnp.concatenate([g10, g11], axis=1)], axis=0
    ) + (MEM - 1.0) * eye
    system[...] = a
    across = lax.rsqrt(jnp.sum(a * eye, axis=0, keepdims=True))
    down = lax.rsqrt(jnp.sum(a * eye, axis=1, keepdims=True))
    x = across * (eye - lower_half(a * across * down - eye))
    rough = x.astype(BF16)
    x = corrected(x, nt(nn(rough, a.astype(BF16)).astype(BF16), rough) - eye)
    inverse[...] = corrected(x, nt3(nn3(x, a), x) - eye)

    def go_on(state):
        step, size = state
        return jnp.logical_and(step < 9, jnp.logical_and(size >= 1e-4, size < 1e6))

    def refine(state):
        step, _ = state
        x = inverse[...]
        residual = nt(nn(x, system[...], HI), x, HI) - eye
        inverse[...] = corrected(x, residual)
        return step + 1, jnp.sum(residual * residual)

    _, size = lax.while_loop(go_on, refine, (jnp.int32(0), jnp.float32(1.0)))

    @pl.when(jnp.logical_not(size < 1e-4))
    def _():
        rows[:, 0:MEM] = system[...]
        rows[:, MEM : 2 * MEM] = eye
        lanes = iota2(1, 2 * MEM, 1)

        def eliminate(j, carry):
            row = rows[pl.ds(j, 1), :]
            pivot = jnp.sum(jnp.where(lanes == j, row, 0.0), axis=1, keepdims=True)
            old = rows[...]
            column = jnp.sum(jnp.where(lanes == j, old, 0.0), axis=1, keepdims=True)
            below = iota2(MEM, 1, 0) > j
            rows[...] = old - jnp.where(below, column / pivot, 0.0) * row
            rows[pl.ds(j, 1), :] = row * (1.0 / jnp.sqrt(pivot))
            return carry

        lax.fori_loop(0, MEM, eliminate, 0)
        inverse[...] = rows[:, MEM : 2 * MEM]

    x = inverse[...]
    last = summed[48]
    pull = jnp.concatenate([last[0:1, :], last[1:2, :]], axis=1)
    halfway = jnp.sum(x * pull, axis=1, keepdims=True)
    target = (MEM - 1.0) ** 0.5 * basis[...] + halfway
    transform = nn3(x.T, target).astype(BF16)
    load.wait()
    copies = []
    for i in range(held.shape[0]):
        size = held.shape[1]
        held[i] = nn(ensemble[i * size : (i + 1) * size, :], transform).astype(BF16)
        copies.append(
            pltpu.make_async_copy(held.at[i], out.at[i * size : (i + 1) * size], sems.at[i])
        )
        copies[-1].start()
    for copy in copies:
        copy.wait()


def send_by(value, axis, steps):
    count = lax.axis_size(axis)
    return lax.ppermute(value, axis, [(s, (s + steps) % count) for s in range(count)])


def swap(x, axis):
    return lax.all_to_all(x, axis, 0, 0, tiled=True)


def summed_everywhere(tiles):
    mine = jnp.sum(swap(tiles, NEAR), axis=0, keepdims=True)
    far = lax.axis_size(FAR)
    mine = jnp.sum(swap(jnp.broadcast_to(mine, (far, 8, 128)), FAR), axis=0, keepdims=True)
    return swap(jnp.broadcast_to(mine, (tiles.shape[0], 8, 128)), NEAR)


def local(
    ensemble,
    jacobian,
    innovation,
    error_vectors,
    error_values,
    ensemble_vectors,
    column_pick,
    footprint_slot,
    footprint_count,
):
    window, capacity = column_pick.shape[1:]
    levels, members = ensemble.shape[1:]
    width = error_vectors.shape[1]
    foot_rows = jacobian.shape[0]
    peers = lax.axis_size(CHAN)
    share = foot_rows // peers
    slab = (levels, members)

    sensitivity = swap(jacobian, CHAN)

    chosen = pl.pallas_call(
        pick_kernel,
        out_shape=[jax.ShapeDtypeStruct((capacity, *slab), BF16)] * window,
        in_specs=[SM, VM],
        out_specs=[VM] * window,
        compiler_params=grant(20),
        cost_estimate=cost(0, 2 * ensemble.size),
        name="pick",
    )(column_pick.reshape(-1), ensemble)
    parts = []
    for o in range(window):
        steps = o - window // 2
        parts.append(send_by(chosen[o], TILE, steps) if steps else chosen[o])

    place = jnp.concatenate(
        [lax.axis_index(CHAN).astype(jnp.int32)[None], footprint_count.astype(jnp.int32)]
    )
    scales = 1.0 / jnp.sqrt(error_values)
    misfits = pl.pallas_call(
        misfit_kernel,
        out_shape=jax.ShapeDtypeStruct((peers, 8, 128), BF16),
        in_specs=[SM, VM, VM, VM],
        out_specs=VM,
        compiler_params=grant(20),
        cost_estimate=cost(2 * foot_rows * width * width, 4 * error_vectors.size),
        name="misfit",
    )(place, innovation, error_vectors, scales.reshape(peers, width))

    payload = pl.pallas_call(
        slot_kernel,
        out_shape=jax.ShapeDtypeStruct((2 * foot_rows + peers, 8, 128), BF16),
        in_specs=[SM] + [VM] * (window + 1),
        out_specs=VM,
        scratch_shapes=[pltpu.VMEM((window * capacity, *slab), BF16)],
        compiler_params=grant(20),
        cost_estimate=cost(0, 4 * foot_rows * levels * members),
        name="slots",
    )(footprint_slot, *parts, misfits)
    payload, sensitivity = lax.optimization_barrier((payload, sensitivity))
    arrived = swap(payload, CHAN)

    turned = pl.pallas_call(
        turn_kernel,
        out_shape=jax.ShapeDtypeStruct((share, peers * width, 128), BF16),
        in_specs=[SM, VM, VM, VM],
        out_specs=VM,
        compiler_params=grant(20),
        cost_estimate=cost(4 * 512 * share * 256 * 128, 4 * jacobian.size),
        name="turn",
    )(place, error_vectors, scales.reshape(2, members), sensitivity)

    tiles = pl.pallas_call(
        terms_kernel,
        out_shape=jax.ShapeDtypeStruct((64, 8, 128), F32),
        in_specs=[VM, VM],
        out_specs=VM,
        compiler_params=grant(20),
        cost_estimate=cost(2 * 512 * share * 256 * 384, 2 * jacobian.size),
        name="terms",
    )(turned, arrived)

    summed = summed_everywhere(tiles)

    chunks = 6
    flat_rows = ensemble.reshape(-1, members)
    updated = pl.pallas_call(
        solve_kernel,
        out_shape=jax.ShapeDtypeStruct(flat_rows.shape, BF16),
        in_specs=[VM, VM, ANY],
        out_specs=ANY,
        scratch_shapes=[
            pltpu.VMEM((members, members), F32),
            pltpu.VMEM((members, members), F32),
            pltpu.VMEM((members, 2 * members), F32),
            pltpu.VMEM(flat_rows.shape, BF16),
            pltpu.VMEM((chunks, flat_rows.shape[0] // chunks, members), BF16),
            pltpu.SemaphoreType.DMA,
            pltpu.SemaphoreType.DMA((chunks,)),
        ],
        compiler_params=grant(53),
        name="solve",
    )(summed, ensemble_vectors, flat_rows)
    return updated.reshape(ensemble.shape)


def solution(mesh):
    finer = Mesh(mesh.devices.reshape(8, 4, 8, 2), ("y", "x", "z", "c"))
    return jax.shard_map(
        local,
        mesh=finer,
        in_specs=(
            P(TILE, CHAN, None),
            P(TILE, CHAN, None),
            P(TILE, CHAN),
            P(),
            P(),
            P(),
            P(TILE, None, None),
            P(TILE),
            P(TILE),
        ),
        out_specs=P(TILE, CHAN, None),
        check_vma=False,
    )
```

```python
import jax
import jax.numpy as jnp
from jax import lax
from jax.experimental import pallas as pl
from jax.experimental.pallas import tpu as pltpu
from jax.sharding import Mesh
from jax.sharding import PartitionSpec as P

TILE = ("y", "x")
CHAN = ("z", "c")
NEAR = ("x", "z", "c")
FAR = "y"
MEM = 256
CHUNK = 7
HI = lax.Precision.HIGHEST
F32 = jnp.float32
BF16 = jnp.bfloat16
VM = pl.BlockSpec(memory_space=pltpu.VMEM)
SM = pl.BlockSpec(memory_space=pltpu.SMEM)
ANY = pl.BlockSpec(memory_space=pl.ANY)


def grant(mebibytes):
    return pltpu.CompilerParams(vmem_limit_bytes=mebibytes * 2**20)


def cost(flops, size):
    return pl.CostEstimate(flops=flops, bytes_accessed=size, transcendentals=0)


def iota2(rows, columns, dim):
    return lax.broadcasted_iota(jnp.int32, (rows, columns), dim)


def nt(a, b, precision=None):
    return lax.dot_general(
        a, b, (((1,), (1,)), ((), ())), precision=precision, preferred_element_type=F32
    )


def nn(a, b, precision=None):
    return lax.dot_general(
        a, b, (((1,), (0,)), ((), ())), precision=precision, preferred_element_type=F32
    )


def split(x):
    high = x.astype(BF16)
    return high, (x - high.astype(F32)).astype(BF16)


def pick_kernel(pick, ensemble, *sends):
    capacity = sends[0].shape[0]
    for o, out in enumerate(sends):

        def one(j, carry, o=o, out=out):
            out[j] = ensemble[pick[o * capacity + j]]
            return carry

        lax.fori_loop(0, capacity, one, 0, unroll=8)


def misfit_kernel(place, innovation, vectors, scales, out):
    group = place[0]
    width = vectors.shape[1]
    start = pl.multiple_of(group * width, width)
    basis = vectors[pl.ds(start, width), :] * scales[pl.ds(group, 1), :]
    misfit = nn(innovation[...], basis, HI)
    peers = out.shape[0]
    share = misfit.shape[0] // peers
    rest = jnp.zeros((16 - share, width), F32)
    blank = jnp.zeros((8, 128 - 2 * width), F32)
    for i in range(peers):
        left = misfit[share * i : share * i + 8, :]
        right = jnp.concatenate([misfit[share * i + 8 : share * (i + 1), :], rest], axis=0)
        out[i] = jnp.concatenate([left, right, blank], axis=1).astype(BF16)


def slot_kernel(slot, a0, a1, a2, a3, a4, misfits, out, held):
    capacity = a0.shape[0]
    for o, part in enumerate((a0, a1, a2, a3, a4)):
        held[o * capacity : (o + 1) * capacity] = part[...]
    peers = misfits.shape[0]
    step = out.shape[0] // peers
    share = step // 2

    def one(i, carry):
        for f in range(share):
            column = held[slot[i * share + f]]
            out[i * step + 2 * f] = column[:, 0:128]
            out[i * step + 2 * f + 1] = column[:, 128:256]
        out[i * step + 2 * share] = misfits[i]
        return carry

    lax.fori_loop(0, peers, one, 0)


def turn_kernel(place, vectors, scales, jacobian, out):
    peers = vectors.shape[0] // vectors.shape[1]
    share = jacobian.shape[0] // peers
    first = place[0] * share
    count = place[1]
    half = MEM
    same = iota2(half, half, 0) // 32 == iota2(half, half, 1) // 32
    turns = []
    for h in range(2):
        block = vectors[h * half : (h + 1) * half, :]
        wide = jnp.where(same, jnp.concatenate([block] * 8, axis=1), 0.0) * scales[h : h + 1, :]
        turns.append(split(wide.T))
    for f in range(share):
        live = jnp.where(first + f < count, 1.0, 0.0).astype(F32)
        for h in range(2):
            block = jnp.concatenate(
                [jacobian[(h * 8 + s) * share + f] for s in range(8)], axis=0
            )
            high, low = turns[h]
            turned = (nn(high, block) + nn(low, block)) * live
            out[f, h * half : (h + 1) * half, :] = turned.astype(BF16)


def terms_kernel(turned, arrived, out):
    share, channels = turned.shape[:2]
    step = 2 * share + 1
    peers = arrived.shape[0] // step
    width = channels // peers
    tiles = [arrived[s * step + 2 * share].astype(F32) for s in range(peers)]
    misfit = [
        jnp.concatenate([t[:, width * k : width * (k + 1)] for t in tiles], axis=1)
        for k in range(2)
    ]
    blank = jnp.zeros((8, channels), F32)
    gram = jnp.zeros((MEM + 16, MEM), F32)
    batch = 5
    for begin in range(0, share, batch):
        lefts, rights = [], []
        for f in range(begin, begin + batch):
            flipped = []
            for h in range(2):
                column = jnp.concatenate(
                    [arrived[s * step + 2 * f + h] for s in range(peers)], axis=0
                )
                flipped.append(column.astype(F32).T.astype(BF16))
            whitened = nt(jnp.concatenate(flipped, axis=0), turned[f]).astype(BF16)
            row = jnp.where(iota2(8, channels, 0) == f % 8, misfit[f // 8], 0.0)
            rows = jnp.concatenate([row, blank], axis=0).astype(BF16)
            rights.append(whitened)
            lefts.append(jnp.concatenate([whitened, rows], axis=0))
        gram = gram + nt(jnp.concatenate(lefts, axis=1), jnp.concatenate(rights, axis=1))
    pull = gram[MEM : MEM + 16, :]
    total = jnp.sum(pull, axis=0, keepdims=True)
    out[0:128, :] = gram[0:128, 0:128]
    out[128:256, :] = gram[128:256, 0:128]
    out[256:384, :] = gram[128:256, 128:256]
    unused = jnp.zeros((out.shape[0] - 386, 128), F32)
    out[384:, :] = jnp.concatenate([total[:, 0:128], total[:, 128:256], unused], axis=0)


def near_sum_kernel(parts, out):
    span = 8 * CHUNK
    x = parts[0:span, :]
    for k in range(1, parts.shape[0] // span):
        x = x + parts[k * span : (k + 1) * span, :]
    y = x[0:CHUNK, :]
    for k in range(1, 8):
        y = y + x[k * CHUNK : (k + 1) * CHUNK, :]
    tile = jnp.concatenate([y, jnp.zeros((8 - CHUNK, 128), F32)], axis=0)
    for k in range(out.shape[0]):
        out[k] = tile


def far_sum_kernel(parts, out):
    y = jnp.sum(parts[...], axis=0)[0:CHUNK, :]
    x = jnp.concatenate([y] * 8, axis=0)
    span = 8 * CHUNK
    for k in range(out.shape[0] // span):
        out[k * span : (k + 1) * span, :] = x


def lower_half(x):
    i, j = iota2(MEM, MEM, 0), iota2(MEM, MEM, 1)
    return jnp.where(i > j, x, jnp.where(i == j, 0.5 * x, 0.0))


def nn3(a, b):
    (ah, al), (bh, bl) = split(a), split(b)
    return nn(ah, bh) + (nn(ah, bl) + nn(al, bh))


def nt3(a, b):
    (ah, al), (bh, bl) = split(a), split(b)
    return nt(ah, bh) + (nt(ah, bl) + nt(al, bh))


def corrected(x, residual):
    return x - nn(lower_half(residual).astype(BF16), x.astype(BF16))


def solve_kernel(
    summed, basis, ensemble_far, out, system, inverse, rows, ensemble, held, load_sem, sems
):
    load = pltpu.make_async_copy(ensemble_far, ensemble, load_sem)
    load.start()
    eye = (iota2(MEM, MEM, 0) == iota2(MEM, MEM, 1)).astype(F32)
    g00 = summed[0:128, :]
    g10 = summed[128:256, :]
    g11 = summed[256:384, :]
    a = jnp.concatenate(
        [jnp.concatenate([g00, g10.T], axis=1), jnp.concatenate([g10, g11], axis=1)], axis=0
    ) + (MEM - 1.0) * eye
    system[...] = a
    across = lax.rsqrt(jnp.sum(a * eye, axis=0, keepdims=True))
    down = lax.rsqrt(jnp.sum(a * eye, axis=1, keepdims=True))
    x = across * (eye - lower_half(a * across * down - eye))
    rough = x.astype(BF16)
    x = corrected(x, nt(nn(rough, a.astype(BF16)).astype(BF16), rough) - eye)
    inverse[...] = corrected(x, nt3(nn3(x, a), x) - eye)

    def go_on(state):
        step, size = state
        return jnp.logical_and(step < 9, jnp.logical_and(size >= 1e-4, size < 1e6))

    def refine(state):
        step, _ = state
        x = inverse[...]
        residual = nt(nn(x, system[...], HI), x, HI) - eye
        inverse[...] = corrected(x, residual)
        return step + 1, jnp.sum(residual * residual)

    _, size = lax.while_loop(go_on, refine, (jnp.int32(0), jnp.float32(1.0)))

    @pl.when(jnp.logical_not(size < 1e-4))
    def _():
        rows[:, 0:MEM] = system[...]
        rows[:, MEM : 2 * MEM] = eye
        lanes = iota2(1, 2 * MEM, 1)

        def eliminate(j, carry):
            row = rows[pl.ds(j, 1), :]
            pivot = jnp.sum(jnp.where(lanes == j, row, 0.0), axis=1, keepdims=True)
            old = rows[...]
            column = jnp.sum(jnp.where(lanes == j, old, 0.0), axis=1, keepdims=True)
            below = iota2(MEM, 1, 0) > j
            rows[...] = old - jnp.where(below, column / pivot, 0.0) * row
            rows[pl.ds(j, 1), :] = row * (1.0 / jnp.sqrt(pivot))
            return carry

        lax.fori_loop(0, MEM, eliminate, 0)
        inverse[...] = rows[:, MEM : 2 * MEM]

    x = inverse[...]
    pull = jnp.concatenate([summed[384:385, :], summed[385:386, :]], axis=1)
    halfway = jnp.sum(x * pull, axis=1, keepdims=True)
    target = (MEM - 1.0) ** 0.5 * basis[...] + halfway
    transform = nn3(x.T, target).astype(BF16)
    load.wait()
    copies = []
    for i in range(held.shape[0]):
        size = held.shape[1]
        held[i] = nn(ensemble[i * size : (i + 1) * size, :], transform).astype(BF16)
        copies.append(
            pltpu.make_async_copy(held.at[i], out.at[i * size : (i + 1) * size], sems.at[i])
        )
        copies[-1].start()
    for copy in copies:
        copy.wait()


def send_by(value, axis, steps):
    count = lax.axis_size(axis)
    return lax.ppermute(value, axis, [(s, (s + steps) % count) for s in range(count)])


def swap(x, axis):
    return lax.all_to_all(x, axis, 0, 0, tiled=True)


def swap_rows(x, axis):
    return swap(x.reshape(-1, 1, 128), axis).reshape(-1, 128)


def summed_everywhere(rows):
    far = lax.axis_size(FAR)
    mine = pl.pallas_call(
        near_sum_kernel,
        out_shape=jax.ShapeDtypeStruct((far, 8, 128), F32),
        in_specs=[VM],
        out_specs=VM,
        compiler_params=grant(20),
        name="near_sum",
    )(swap_rows(rows, NEAR))
    mine = pl.pallas_call(
        far_sum_kernel,
        out_shape=jax.ShapeDtypeStruct(rows.shape, F32),
        in_specs=[VM],
        out_specs=VM,
        compiler_params=grant(20),
        name="far_sum",
    )(swap(mine, FAR))
    return swap_rows(mine, NEAR)


def local(
    ensemble,
    jacobian,
    innovation,
    error_vectors,
    error_values,
    ensemble_vectors,
    column_pick,
    footprint_slot,
    footprint_count,
):
    window, capacity = column_pick.shape[1:]
    levels, members = ensemble.shape[1:]
    width = error_vectors.shape[1]
    foot_rows = jacobian.shape[0]
    peers = lax.axis_size(CHAN)
    share = foot_rows // peers
    slab = (levels, members)

    sensitivity = swap(jacobian, CHAN)

    chosen = pl.pallas_call(
        pick_kernel,
        out_shape=[jax.ShapeDtypeStruct((capacity, *slab), BF16)] * window,
        in_specs=[SM, VM],
        out_specs=[VM] * window,
        compiler_params=grant(20),
        cost_estimate=cost(0, 2 * ensemble.size),
        name="pick",
    )(column_pick.reshape(-1), ensemble)
    parts = []
    for o in range(window):
        steps = o - window // 2
        parts.append(send_by(chosen[o], TILE, steps) if steps else chosen[o])

    place = jnp.concatenate(
        [lax.axis_index(CHAN).astype(jnp.int32)[None], footprint_count.astype(jnp.int32)]
    )
    scales = 1.0 / jnp.sqrt(error_values)
    misfits = pl.pallas_call(
        misfit_kernel,
        out_shape=jax.ShapeDtypeStruct((peers, 8, 128), BF16),
        in_specs=[SM, VM, VM, VM],
        out_specs=VM,
        compiler_params=grant(20),
        cost_estimate=cost(2 * foot_rows * width * width, 4 * error_vectors.size),
        name="misfit",
    )(place, innovation, error_vectors, scales.reshape(peers, width))

    payload = pl.pallas_call(
        slot_kernel,
        out_shape=jax.ShapeDtypeStruct((2 * foot_rows + peers, 8, 128), BF16),
        in_specs=[SM] + [VM] * (window + 1),
        out_specs=VM,
        scratch_shapes=[pltpu.VMEM((window * capacity, *slab), BF16)],
        compiler_params=grant(20),
        cost_estimate=cost(0, 4 * foot_rows * levels * members),
        name="slots",
    )(footprint_slot, *parts, misfits)
    payload, sensitivity = lax.optimization_barrier((payload, sensitivity))
    arrived = swap(payload, CHAN)

    turned = pl.pallas_call(
        turn_kernel,
        out_shape=jax.ShapeDtypeStruct((share, peers * width, 128), BF16),
        in_specs=[SM, VM, VM, VM],
        out_specs=VM,
        compiler_params=grant(20),
        cost_estimate=cost(4 * 512 * share * 256 * 128, 4 * jacobian.size),
        name="turn",
    )(place, error_vectors, scales.reshape(2, members), sensitivity)

    tiles = pl.pallas_call(
        terms_kernel,
        out_shape=jax.ShapeDtypeStruct((64 * CHUNK, 128), F32),
        in_specs=[VM, VM],
        out_specs=VM,
        compiler_params=grant(20),
        cost_estimate=cost(2 * 512 * share * 256 * 384, 2 * jacobian.size),
        name="terms",
    )(turned, arrived)

    summed = summed_everywhere(tiles)

    chunks = 6
    flat_rows = ensemble.reshape(-1, members)
    updated = pl.pallas_call(
        solve_kernel,
        out_shape=jax.ShapeDtypeStruct(flat_rows.shape, BF16),
        in_specs=[VM, VM, ANY],
        out_specs=ANY,
        scratch_shapes=[
            pltpu.VMEM((members, members), F32),
            pltpu.VMEM((members, members), F32),
            pltpu.VMEM((members, 2 * members), F32),
            pltpu.VMEM(flat_rows.shape, BF16),
            pltpu.VMEM((chunks, flat_rows.shape[0] // chunks, members), BF16),
            pltpu.SemaphoreType.DMA,
            pltpu.SemaphoreType.DMA((chunks,)),
        ],
        compiler_params=grant(53),
        name="solve",
    )(summed, ensemble_vectors, flat_rows)
    return updated.reshape(ensemble.shape)


def solution(mesh):
    finer = Mesh(mesh.devices.reshape(8, 4, 8, 2), ("y", "x", "z", "c"))
    return jax.shard_map(
        local,
        mesh=finer,
        in_specs=(
            P(TILE, CHAN, None),
            P(TILE, CHAN, None),
            P(TILE, CHAN),
            P(),
            P(),
            P(),
            P(TILE, None, None),
            P(TILE),
            P(TILE),
        ),
        out_specs=P(TILE, CHAN, None),
        check_vma=False,
    )
```

```python
import jax
import jax.numpy as jnp
from jax import lax
from jax.experimental import pallas as pl
from jax.experimental.pallas import tpu as pltpu
from jax.sharding import Mesh
from jax.sharding import PartitionSpec as P

TILE = ("y", "x")
CHAN = ("z", "c")
NEAR = ("x", "z", "c")
FAR = "y"
MEM = 256
CHUNK = 5
HI = lax.Precision.HIGHEST
F32 = jnp.float32
BF16 = jnp.bfloat16
VM = pl.BlockSpec(memory_space=pltpu.VMEM)
SM = pl.BlockSpec(memory_space=pltpu.SMEM)
ANY = pl.BlockSpec(memory_space=pl.ANY)


def grant(mebibytes):
    return pltpu.CompilerParams(vmem_limit_bytes=mebibytes * 2**20)


def cost(flops, size):
    return pl.CostEstimate(flops=flops, bytes_accessed=size, transcendentals=0)


def iota2(rows, columns, dim):
    return lax.broadcasted_iota(jnp.int32, (rows, columns), dim)


def nt(a, b, precision=None):
    return lax.dot_general(
        a, b, (((1,), (1,)), ((), ())), precision=precision, preferred_element_type=F32
    )


def nn(a, b, precision=None):
    return lax.dot_general(
        a, b, (((1,), (0,)), ((), ())), precision=precision, preferred_element_type=F32
    )


def split(x):
    high = x.astype(BF16)
    return high, (x - high.astype(F32)).astype(BF16)


def pick_kernel(pick, ensemble, *sends):
    capacity = sends[0].shape[0]
    for o, out in enumerate(sends):

        def one(j, carry, o=o, out=out):
            out[j] = ensemble[pick[o * capacity + j]]
            return carry

        lax.fori_loop(0, capacity, one, 0, unroll=8)


def misfit_kernel(place, innovation, vectors, scales, out):
    group = place[0]
    width = vectors.shape[1]
    start = pl.multiple_of(group * width, width)
    basis = vectors[pl.ds(start, width), :] * scales[pl.ds(group, 1), :]
    misfit = nn(innovation[...], basis, HI)
    peers = out.shape[0]
    share = misfit.shape[0] // peers
    rest = jnp.zeros((16 - share, width), F32)
    blank = jnp.zeros((8, 128 - 2 * width), F32)
    for i in range(peers):
        left = misfit[share * i : share * i + 8, :]
        right = jnp.concatenate([misfit[share * i + 8 : share * (i + 1), :], rest], axis=0)
        out[i] = jnp.concatenate([left, right, blank], axis=1).astype(BF16)


def slot_kernel(slot, a0, a1, a2, a3, a4, misfits, out, held):
    capacity = a0.shape[0]
    for o, part in enumerate((a0, a1, a2, a3, a4)):
        held[o * capacity : (o + 1) * capacity] = part[...]
    peers = misfits.shape[0]
    step = out.shape[0] // peers
    share = step // 2

    def one(i, carry):
        for f in range(share):
            column = held[slot[i * share + f]]
            out[i * step + 2 * f] = column[:, 0:128]
            out[i * step + 2 * f + 1] = column[:, 128:256]
        out[i * step + 2 * share] = misfits[i]
        return carry

    lax.fori_loop(0, peers, one, 0)


def turn_kernel(place, vectors, scales, jacobian, out):
    peers = vectors.shape[0] // vectors.shape[1]
    share = jacobian.shape[0] // peers
    first = place[0] * share
    count = place[1]
    half = MEM
    same = iota2(half, half, 0) // 32 == iota2(half, half, 1) // 32
    turns = []
    for h in range(2):
        block = vectors[h * half : (h + 1) * half, :]
        wide = jnp.where(same, jnp.concatenate([block] * 8, axis=1), 0.0) * scales[h : h + 1, :]
        turns.append(split(wide.T))
    for f in range(share):
        live = jnp.where(first + f < count, 1.0, 0.0).astype(F32)
        for h in range(2):
            block = jnp.concatenate(
                [jacobian[(h * 8 + s) * share + f] for s in range(8)], axis=0
            )
            high, low = turns[h]
            turned = (nn(high, block) + nn(low, block)) * live
            out[f, h * half : (h + 1) * half, :] = turned.astype(BF16)


def terms_kernel(turned, arrived, out):
    share, channels = turned.shape[:2]
    step = 2 * share + 1
    peers = arrived.shape[0] // step
    width = channels // peers
    tiles = [arrived[s * step + 2 * share].astype(F32) for s in range(peers)]
    misfit = [
        jnp.concatenate([t[:, width * k : width * (k + 1)] for t in tiles], axis=1)
        for k in range(2)
    ]
    blank = jnp.zeros((8, channels), F32)
    gram = jnp.zeros((MEM + 16, MEM), F32)
    batch = 5
    for begin in range(0, share, batch):
        lefts, rights = [], []
        for f in range(begin, begin + batch):
            flipped = []
            for h in range(2):
                column = jnp.concatenate(
                    [arrived[s * step + 2 * f + h] for s in range(peers)], axis=0
                )
                flipped.append(column.astype(F32).T.astype(BF16))
            whitened = nt(jnp.concatenate(flipped, axis=0), turned[f]).astype(BF16)
            row = jnp.where(iota2(8, channels, 0) == f % 8, misfit[f // 8], 0.0)
            rows = jnp.concatenate([row, blank], axis=0).astype(BF16)
            rights.append(whitened)
            lefts.append(jnp.concatenate([whitened, rows], axis=0))
        gram = gram + nt(jnp.concatenate(lefts, axis=1), jnp.concatenate(rights, axis=1))
    pull = gram[MEM : MEM + 16, :]
    total = jnp.sum(pull, axis=0, keepdims=True)
    row, col = iota2(128, 128, 0), iota2(128, 128, 1)
    other = gram[128:256, 128:256]
    out[0:128, :] = jnp.where(row >= col, gram[0:128, 0:128], other)
    out[128:256, :] = gram[128:256, 0:128]
    diagonal = jnp.sum(jnp.where(row == col, other, 0.0), axis=0, keepdims=True)
    unused = jnp.zeros((out.shape[0] - 259, 128), F32)
    out[256:, :] = jnp.concatenate(
        [diagonal, total[:, 0:128], total[:, 128:256], unused], axis=0
    )


def near_sum_kernel(parts, out):
    span = 8 * CHUNK
    x = parts[0:span, :]
    for k in range(1, parts.shape[0] // span):
        x = x + parts[k * span : (k + 1) * span, :]
    y = x[0:CHUNK, :]
    for k in range(1, 8):
        y = y + x[k * CHUNK : (k + 1) * CHUNK, :]
    tile = jnp.concatenate([y, jnp.zeros((8 - CHUNK, 128), F32)], axis=0)
    for k in range(out.shape[0]):
        out[k] = tile


def far_sum_kernel(parts, out):
    y = jnp.sum(parts[...], axis=0)[0:CHUNK, :]
    x = jnp.concatenate([y] * 8, axis=0)
    span = 8 * CHUNK
    for k in range(out.shape[0] // span):
        out[k * span : (k + 1) * span, :] = x


def lower_half(x):
    i, j = iota2(MEM, MEM, 0), iota2(MEM, MEM, 1)
    return jnp.where(i > j, x, jnp.where(i == j, 0.5 * x, 0.0))


def nn3(a, b):
    (ah, al), (bh, bl) = split(a), split(b)
    return nn(ah, bh) + (nn(ah, bl) + nn(al, bh))


def nt3(a, b):
    (ah, al), (bh, bl) = split(a), split(b)
    return nt(ah, bh) + (nt(ah, bl) + nt(al, bh))


def corrected(x, residual):
    return x - nn(lower_half(residual).astype(BF16), x.astype(BF16))


def solve_kernel(
    summed, basis, ensemble_far, out, system, inverse, rows, ensemble, held, load_sem, sems
):
    load = pltpu.make_async_copy(ensemble_far, ensemble, load_sem)
    load.start()
    eye = (iota2(MEM, MEM, 0) == iota2(MEM, MEM, 1)).astype(F32)
    row, col = iota2(128, 128, 0), iota2(128, 128, 1)
    shared = summed[0:128, :]
    below = jnp.where(row > col, shared, 0.0)
    above = jnp.where(row < col, shared, 0.0)
    g00 = below + below.T + jnp.where(row == col, shared, 0.0)
    g11 = above + above.T + jnp.where(row == col, summed[256:257, :], 0.0)
    g10 = summed[128:256, :]
    a = jnp.concatenate(
        [jnp.concatenate([g00, g10.T], axis=1), jnp.concatenate([g10, g11], axis=1)], axis=0
    ) + (MEM - 1.0) * eye
    system[...] = a
    across = lax.rsqrt(jnp.sum(a * eye, axis=0, keepdims=True))
    down = lax.rsqrt(jnp.sum(a * eye, axis=1, keepdims=True))
    x = across * (eye - lower_half(a * across * down - eye))
    rough = x.astype(BF16)
    x = corrected(x, nt(nn(rough, a.astype(BF16)).astype(BF16), rough) - eye)
    inverse[...] = corrected(x, nt3(nn3(x, a), x) - eye)

    def go_on(state):
        step, size = state
        return jnp.logical_and(step < 9, jnp.logical_and(size >= 1e-4, size < 1e6))

    def refine(state):
        step, _ = state
        x = inverse[...]
        residual = nt(nn(x, system[...], HI), x, HI) - eye
        inverse[...] = corrected(x, residual)
        return step + 1, jnp.sum(residual * residual)

    _, size = lax.while_loop(go_on, refine, (jnp.int32(0), jnp.float32(1.0)))

    @pl.when(jnp.logical_not(size < 1e-4))
    def _():
        rows[:, 0:MEM] = system[...]
        rows[:, MEM : 2 * MEM] = eye
        lanes = iota2(1, 2 * MEM, 1)

        def eliminate(j, carry):
            row = rows[pl.ds(j, 1), :]
            pivot = jnp.sum(jnp.where(lanes == j, row, 0.0), axis=1, keepdims=True)
            old = rows[...]
            column = jnp.sum(jnp.where(lanes == j, old, 0.0), axis=1, keepdims=True)
            below = iota2(MEM, 1, 0) > j
            rows[...] = old - jnp.where(below, column / pivot, 0.0) * row
            rows[pl.ds(j, 1), :] = row * (1.0 / jnp.sqrt(pivot))
            return carry

        lax.fori_loop(0, MEM, eliminate, 0)
        inverse[...] = rows[:, MEM : 2 * MEM]

    x = inverse[...]
    pull = jnp.concatenate([summed[257:258, :], summed[258:259, :]], axis=1)
    halfway = jnp.sum(x * pull, axis=1, keepdims=True)
    target = (MEM - 1.0) ** 0.5 * basis[...] + halfway
    transform = nn3(x.T, target).astype(BF16)
    load.wait()
    copies = []
    for i in range(held.shape[0]):
        size = held.shape[1]
        held[i] = nn(ensemble[i * size : (i + 1) * size, :], transform).astype(BF16)
        copies.append(
            pltpu.make_async_copy(held.at[i], out.at[i * size : (i + 1) * size], sems.at[i])
        )
        copies[-1].start()
    for copy in copies:
        copy.wait()


def send_by(value, axis, steps):
    count = lax.axis_size(axis)
    return lax.ppermute(value, axis, [(s, (s + steps) % count) for s in range(count)])


def swap(x, axis):
    return lax.all_to_all(x, axis, 0, 0, tiled=True)


def swap_rows(x, axis):
    return swap(x.reshape(-1, 1, 128), axis).reshape(-1, 128)


def summed_everywhere(rows):
    far = lax.axis_size(FAR)
    mine = pl.pallas_call(
        near_sum_kernel,
        out_shape=jax.ShapeDtypeStruct((far, 8, 128), F32),
        in_specs=[VM],
        out_specs=VM,
        compiler_params=grant(20),
        name="near_sum",
    )(swap_rows(rows, NEAR))
    mine = pl.pallas_call(
        far_sum_kernel,
        out_shape=jax.ShapeDtypeStruct(rows.shape, F32),
        in_specs=[VM],
        out_specs=VM,
        compiler_params=grant(20),
        name="far_sum",
    )(swap(mine, FAR))
    return swap_rows(mine, NEAR)


def local(
    ensemble,
    jacobian,
    innovation,
    error_vectors,
    error_values,
    ensemble_vectors,
    column_pick,
    footprint_slot,
    footprint_count,
):
    window, capacity = column_pick.shape[1:]
    levels, members = ensemble.shape[1:]
    width = error_vectors.shape[1]
    foot_rows = jacobian.shape[0]
    peers = lax.axis_size(CHAN)
    share = foot_rows // peers
    slab = (levels, members)

    sensitivity = swap(jacobian, CHAN)

    chosen = pl.pallas_call(
        pick_kernel,
        out_shape=[jax.ShapeDtypeStruct((capacity, *slab), BF16)] * window,
        in_specs=[SM, VM],
        out_specs=[VM] * window,
        compiler_params=grant(20),
        cost_estimate=cost(0, 2 * ensemble.size),
        name="pick",
    )(column_pick.reshape(-1), ensemble)
    parts = []
    for o in range(window):
        steps = o - window // 2
        parts.append(send_by(chosen[o], TILE, steps) if steps else chosen[o])

    place = jnp.concatenate(
        [lax.axis_index(CHAN).astype(jnp.int32)[None], footprint_count.astype(jnp.int32)]
    )
    scales = 1.0 / jnp.sqrt(error_values)
    misfits = pl.pallas_call(
        misfit_kernel,
        out_shape=jax.ShapeDtypeStruct((peers, 8, 128), BF16),
        in_specs=[SM, VM, VM, VM],
        out_specs=VM,
        compiler_params=grant(20),
        cost_estimate=cost(2 * foot_rows * width * width, 4 * error_vectors.size),
        name="misfit",
    )(place, innovation, error_vectors, scales.reshape(peers, width))

    payload = pl.pallas_call(
        slot_kernel,
        out_shape=jax.ShapeDtypeStruct((2 * foot_rows + peers, 8, 128), BF16),
        in_specs=[SM] + [VM] * (window + 1),
        out_specs=VM,
        scratch_shapes=[pltpu.VMEM((window * capacity, *slab), BF16)],
        compiler_params=grant(20),
        cost_estimate=cost(0, 4 * foot_rows * levels * members),
        name="slots",
    )(footprint_slot, *parts, misfits)
    payload, sensitivity = lax.optimization_barrier((payload, sensitivity))
    arrived = swap(payload, CHAN)

    turned = pl.pallas_call(
        turn_kernel,
        out_shape=jax.ShapeDtypeStruct((share, peers * width, 128), BF16),
        in_specs=[SM, VM, VM, VM],
        out_specs=VM,
        compiler_params=grant(20),
        cost_estimate=cost(4 * 512 * share * 256 * 128, 4 * jacobian.size),
        name="turn",
    )(place, error_vectors, scales.reshape(2, members), sensitivity)

    tiles = pl.pallas_call(
        terms_kernel,
        out_shape=jax.ShapeDtypeStruct((64 * CHUNK, 128), F32),
        in_specs=[VM, VM],
        out_specs=VM,
        compiler_params=grant(20),
        cost_estimate=cost(2 * 512 * share * 256 * 384, 2 * jacobian.size),
        name="terms",
    )(turned, arrived)

    summed = summed_everywhere(tiles)

    chunks = 6
    flat_rows = ensemble.reshape(-1, members)
    updated = pl.pallas_call(
        solve_kernel,
        out_shape=jax.ShapeDtypeStruct(flat_rows.shape, BF16),
        in_specs=[VM, VM, ANY],
        out_specs=ANY,
        scratch_shapes=[
            pltpu.VMEM((members, members), F32),
            pltpu.VMEM((members, members), F32),
            pltpu.VMEM((members, 2 * members), F32),
            pltpu.VMEM(flat_rows.shape, BF16),
            pltpu.VMEM((chunks, flat_rows.shape[0] // chunks, members), BF16),
            pltpu.SemaphoreType.DMA,
            pltpu.SemaphoreType.DMA((chunks,)),
        ],
        compiler_params=grant(53),
        name="solve",
    )(summed, ensemble_vectors, flat_rows)
    return updated.reshape(ensemble.shape)


def solution(mesh):
    finer = Mesh(mesh.devices.reshape(8, 4, 8, 2), ("y", "x", "z", "c"))
    return jax.shard_map(
        local,
        mesh=finer,
        in_specs=(
            P(TILE, CHAN, None),
            P(TILE, CHAN, None),
            P(TILE, CHAN),
            P(),
            P(),
            P(),
            P(TILE, None, None),
            P(TILE),
            P(TILE),
        ),
        out_specs=P(TILE, CHAN, None),
        check_vma=False,
    )
```

```python
import jax
import jax.numpy as jnp
from jax import lax
from jax.experimental import pallas as pl
from jax.experimental.pallas import tpu as pltpu
from jax.sharding import Mesh
from jax.sharding import PartitionSpec as P

TILE = ("y", "x")
CHAN = ("z", "c")
NEAR = ("x", "z", "c")
FAR = "y"
MEM = 256
CHUNK = 5
HI = lax.Precision.HIGHEST
F32 = jnp.float32
BF16 = jnp.bfloat16
VM = pl.BlockSpec(memory_space=pltpu.VMEM)
SM = pl.BlockSpec(memory_space=pltpu.SMEM)
ANY = pl.BlockSpec(memory_space=pl.ANY)


def grant(mebibytes):
    return pltpu.CompilerParams(vmem_limit_bytes=mebibytes * 2**20)


def cost(flops, size):
    return pl.CostEstimate(flops=flops, bytes_accessed=size, transcendentals=0)


def iota2(rows, columns, dim):
    return lax.broadcasted_iota(jnp.int32, (rows, columns), dim)


def nt(a, b, precision=None):
    return lax.dot_general(
        a, b, (((1,), (1,)), ((), ())), precision=precision, preferred_element_type=F32
    )


def nn(a, b, precision=None):
    return lax.dot_general(
        a, b, (((1,), (0,)), ((), ())), precision=precision, preferred_element_type=F32
    )


def split(x):
    high = x.astype(BF16)
    return high, (x - high.astype(F32)).astype(BF16)


def pick_kernel(pick, ensemble, *sends):
    capacity = sends[0].shape[0]
    for o, out in enumerate(sends):

        def one(j, carry, o=o, out=out):
            out[j] = ensemble[pick[o * capacity + j]]
            return carry

        lax.fori_loop(0, capacity, one, 0, unroll=8)


def misfit_kernel(place, innovation, vectors, scales, out):
    group = place[0]
    width = vectors.shape[1]
    start = pl.multiple_of(group * width, width)
    basis = vectors[pl.ds(start, width), :] * scales[pl.ds(group, 1), :]
    misfit = nn(innovation[...], basis, HI)
    peers = out.shape[0]
    share = misfit.shape[0] // peers
    rest = jnp.zeros((16 - share, width), F32)
    blank = jnp.zeros((8, 128 - 2 * width), F32)
    for i in range(peers):
        left = misfit[share * i : share * i + 8, :]
        right = jnp.concatenate([misfit[share * i + 8 : share * (i + 1), :], rest], axis=0)
        out[i] = jnp.concatenate([left, right, blank], axis=1).astype(BF16)


def slot_kernel(slot, a0, a1, a2, a3, a4, misfits, out, held):
    capacity = a0.shape[0]
    for o, part in enumerate((a0, a1, a2, a3, a4)):
        held[o * capacity : (o + 1) * capacity] = part[...]
    peers = misfits.shape[0]
    step = out.shape[0] // peers
    share = step // 2

    def one(i, carry):
        for f in range(share):
            column = held[slot[i * share + f]]
            out[i * step + 2 * f] = column[:, 0:128]
            out[i * step + 2 * f + 1] = column[:, 128:256]
        out[i * step + 2 * share] = misfits[i]
        return carry

    lax.fori_loop(0, peers, one, 0)


def turn_kernel(place, vectors, scales, jacobian, out):
    peers = vectors.shape[0] // vectors.shape[1]
    share = jacobian.shape[0] // peers
    first = place[0] * share
    count = place[1]
    half = MEM
    same = iota2(half, half, 0) // 32 == iota2(half, half, 1) // 32
    turns = []
    for h in range(2):
        block = vectors[h * half : (h + 1) * half, :]
        wide = jnp.where(same, jnp.concatenate([block] * 8, axis=1), 0.0) * scales[h : h + 1, :]
        turns.append(split(wide.T))
    for f in range(share):
        live = jnp.where(first + f < count, 1.0, 0.0).astype(F32)
        for h in range(2):
            block = jnp.concatenate(
                [jacobian[(h * 8 + s) * share + f] for s in range(8)], axis=0
            )
            high, low = turns[h]
            turned = (nn(high, block) + nn(low, block)) * live
            out[f, h * half : (h + 1) * half, :] = turned.astype(BF16)


def terms_kernel(turned, arrived, out):
    share, channels = turned.shape[:2]
    step = 2 * share + 1
    peers = arrived.shape[0] // step
    width = channels // peers
    tiles = [arrived[s * step + 2 * share].astype(F32) for s in range(peers)]
    misfit = [
        jnp.concatenate([t[:, width * k : width * (k + 1)] for t in tiles], axis=1)
        for k in range(2)
    ]
    blank = jnp.zeros((8, channels), F32)
    gram = jnp.zeros((MEM + 16, MEM), F32)
    batch = 5
    for begin in range(0, share, batch):
        lefts, rights = [], []
        for f in range(begin, begin + batch):
            flipped = []
            for h in range(2):
                column = jnp.concatenate(
                    [arrived[s * step + 2 * f + h] for s in range(peers)], axis=0
                )
                flipped.append(column.astype(F32).T.astype(BF16))
            whitened = nt(jnp.concatenate(flipped, axis=0), turned[f]).astype(BF16)
            row = jnp.where(iota2(8, channels, 0) == f % 8, misfit[f // 8], 0.0)
            rows = jnp.concatenate([row, blank], axis=0).astype(BF16)
            rights.append(whitened)
            lefts.append(jnp.concatenate([whitened, rows], axis=0))
        gram = gram + nt(jnp.concatenate(lefts, axis=1), jnp.concatenate(rights, axis=1))
    pull = gram[MEM : MEM + 16, :]
    total = jnp.sum(pull, axis=0, keepdims=True)
    row, col = iota2(128, 128, 0), iota2(128, 128, 1)
    other = gram[128:256, 128:256]
    out[0:128, :] = jnp.where(row >= col, gram[0:128, 0:128], other)
    out[128:256, :] = gram[128:256, 0:128]
    diagonal = jnp.sum(jnp.where(row == col, other, 0.0), axis=0, keepdims=True)
    unused = jnp.zeros((out.shape[0] - 259, 128), F32)
    out[256:, :] = jnp.concatenate(
        [diagonal, total[:, 0:128], total[:, 128:256], unused], axis=0
    )


def near_sum_kernel(parts, out):
    span = 8 * CHUNK
    x = parts[0:span, :]
    for k in range(1, parts.shape[0] // span):
        x = x + parts[k * span : (k + 1) * span, :]
    y = x[0:CHUNK, :]
    for k in range(1, 8):
        y = y + x[k * CHUNK : (k + 1) * CHUNK, :]
    out[...] = jnp.concatenate([y] * (out.shape[0] // CHUNK), axis=0)


def far_sum_kernel(parts, out):
    y = parts[0:CHUNK, :]
    for k in range(1, parts.shape[0] // CHUNK):
        y = y + parts[k * CHUNK : (k + 1) * CHUNK, :]
    x = jnp.concatenate([y] * 8, axis=0)
    span = 8 * CHUNK
    for k in range(out.shape[0] // span):
        out[k * span : (k + 1) * span, :] = x


def lower_half(x):
    i, j = iota2(MEM, MEM, 0), iota2(MEM, MEM, 1)
    return jnp.where(i > j, x, jnp.where(i == j, 0.5 * x, 0.0))


def nn3(a, b):
    (ah, al), (bh, bl) = split(a), split(b)
    return nn(ah, bh) + (nn(ah, bl) + nn(al, bh))


def nt3(a, b):
    (ah, al), (bh, bl) = split(a), split(b)
    return nt(ah, bh) + (nt(ah, bl) + nt(al, bh))


def corrected(x, residual):
    return x - nn(lower_half(residual).astype(BF16), x.astype(BF16))


def solve_kernel(
    summed, basis, ensemble_far, out, system, inverse, rows, ensemble, held, load_sem, sems
):
    load = pltpu.make_async_copy(ensemble_far, ensemble, load_sem)
    load.start()
    eye = (iota2(MEM, MEM, 0) == iota2(MEM, MEM, 1)).astype(F32)
    row, col = iota2(128, 128, 0), iota2(128, 128, 1)
    shared = summed[0:128, :]
    below = jnp.where(row > col, shared, 0.0)
    above = jnp.where(row < col, shared, 0.0)
    g00 = below + below.T + jnp.where(row == col, shared, 0.0)
    g11 = above + above.T + jnp.where(row == col, summed[256:257, :], 0.0)
    g10 = summed[128:256, :]
    a = jnp.concatenate(
        [jnp.concatenate([g00, g10.T], axis=1), jnp.concatenate([g10, g11], axis=1)], axis=0
    ) + (MEM - 1.0) * eye
    system[...] = a
    across = lax.rsqrt(jnp.sum(a * eye, axis=0, keepdims=True))
    down = lax.rsqrt(jnp.sum(a * eye, axis=1, keepdims=True))
    x = across * (eye - lower_half(a * across * down - eye))
    rough = x.astype(BF16)
    x = corrected(x, nt(nn(rough, a.astype(BF16)).astype(BF16), rough) - eye)
    inverse[...] = corrected(x, nt3(nn3(x, a), x) - eye)

    def go_on(state):
        step, size = state
        return jnp.logical_and(step < 9, jnp.logical_and(size >= 1e-4, size < 1e6))

    def refine(state):
        step, _ = state
        x = inverse[...]
        residual = nt(nn(x, system[...], HI), x, HI) - eye
        inverse[...] = corrected(x, residual)
        return step + 1, jnp.sum(residual * residual)

    _, size = lax.while_loop(go_on, refine, (jnp.int32(0), jnp.float32(1.0)))

    @pl.when(jnp.logical_not(size < 1e-4))
    def _():
        rows[:, 0:MEM] = system[...]
        rows[:, MEM : 2 * MEM] = eye
        lanes = iota2(1, 2 * MEM, 1)

        def eliminate(j, carry):
            row = rows[pl.ds(j, 1), :]
            pivot = jnp.sum(jnp.where(lanes == j, row, 0.0), axis=1, keepdims=True)
            old = rows[...]
            column = jnp.sum(jnp.where(lanes == j, old, 0.0), axis=1, keepdims=True)
            below = iota2(MEM, 1, 0) > j
            rows[...] = old - jnp.where(below, column / pivot, 0.0) * row
            rows[pl.ds(j, 1), :] = row * (1.0 / jnp.sqrt(pivot))
            return carry

        lax.fori_loop(0, MEM, eliminate, 0)
        inverse[...] = rows[:, MEM : 2 * MEM]

    x = inverse[...]
    pull = jnp.concatenate([summed[257:258, :], summed[258:259, :]], axis=1)
    halfway = jnp.sum(x * pull, axis=1, keepdims=True)
    target = (MEM - 1.0) ** 0.5 * basis[...] + halfway
    transform = nn3(x.T, target).astype(BF16)
    load.wait()
    copies = []
    for i in range(held.shape[0]):
        size = held.shape[1]
        held[i] = nn(ensemble[i * size : (i + 1) * size, :], transform).astype(BF16)
        copies.append(
            pltpu.make_async_copy(held.at[i], out.at[i * size : (i + 1) * size], sems.at[i])
        )
        copies[-1].start()
    for copy in copies:
        copy.wait()


def send_by(value, axis, steps):
    count = lax.axis_size(axis)
    return lax.ppermute(value, axis, [(s, (s + steps) % count) for s in range(count)])


def swap(x, axis):
    return lax.all_to_all(x, axis, 0, 0, tiled=True)


def swap_rows(x, axis):
    return swap(x.reshape(-1, 1, 128), axis).reshape(-1, 128)


def summed_everywhere(rows):
    far = lax.axis_size(FAR)
    mine = pl.pallas_call(
        near_sum_kernel,
        out_shape=jax.ShapeDtypeStruct((far * CHUNK, 128), F32),
        in_specs=[VM],
        out_specs=VM,
        compiler_params=grant(20),
        name="near_sum",
    )(swap_rows(rows, NEAR))
    mine = pl.pallas_call(
        far_sum_kernel,
        out_shape=jax.ShapeDtypeStruct(rows.shape, F32),
        in_specs=[VM],
        out_specs=VM,
        compiler_params=grant(20),
        name="far_sum",
    )(swap_rows(mine, FAR))
    return swap_rows(mine, NEAR)


def local(
    ensemble,
    jacobian,
    innovation,
    error_vectors,
    error_values,
    ensemble_vectors,
    column_pick,
    footprint_slot,
    footprint_count,
):
    window, capacity = column_pick.shape[1:]
    levels, members = ensemble.shape[1:]
    width = error_vectors.shape[1]
    foot_rows = jacobian.shape[0]
    peers = lax.axis_size(CHAN)
    share = foot_rows // peers
    slab = (levels, members)

    sensitivity = swap(jacobian, CHAN)

    chosen = pl.pallas_call(
        pick_kernel,
        out_shape=[jax.ShapeDtypeStruct((capacity, *slab), BF16)] * window,
        in_specs=[SM, VM],
        out_specs=[VM] * window,
        compiler_params=grant(20),
        cost_estimate=cost(0, 2 * ensemble.size),
        name="pick",
    )(column_pick.reshape(-1), ensemble)
    parts = []
    for o in range(window):
        steps = o - window // 2
        parts.append(send_by(chosen[o], TILE, steps) if steps else chosen[o])

    place = jnp.concatenate(
        [lax.axis_index(CHAN).astype(jnp.int32)[None], footprint_count.astype(jnp.int32)]
    )
    scales = 1.0 / jnp.sqrt(error_values)
    misfits = pl.pallas_call(
        misfit_kernel,
        out_shape=jax.ShapeDtypeStruct((peers, 8, 128), BF16),
        in_specs=[SM, VM, VM, VM],
        out_specs=VM,
        compiler_params=grant(20),
        cost_estimate=cost(2 * foot_rows * width * width, 4 * error_vectors.size),
        name="misfit",
    )(place, innovation, error_vectors, scales.reshape(peers, width))

    payload = pl.pallas_call(
        slot_kernel,
        out_shape=jax.ShapeDtypeStruct((2 * foot_rows + peers, 8, 128), BF16),
        in_specs=[SM] + [VM] * (window + 1),
        out_specs=VM,
        scratch_shapes=[pltpu.VMEM((window * capacity, *slab), BF16)],
        compiler_params=grant(20),
        cost_estimate=cost(0, 4 * foot_rows * levels * members),
        name="slots",
    )(footprint_slot, *parts, misfits)
    payload, sensitivity = lax.optimization_barrier((payload, sensitivity))
    arrived = swap(payload, CHAN)

    turned = pl.pallas_call(
        turn_kernel,
        out_shape=jax.ShapeDtypeStruct((share, peers * width, 128), BF16),
        in_specs=[SM, VM, VM, VM],
        out_specs=VM,
        compiler_params=grant(20),
        cost_estimate=cost(4 * 512 * share * 256 * 128, 4 * jacobian.size),
        name="turn",
    )(place, error_vectors, scales.reshape(2, members), sensitivity)

    tiles = pl.pallas_call(
        terms_kernel,
        out_shape=jax.ShapeDtypeStruct((64 * CHUNK, 128), F32),
        in_specs=[VM, VM],
        out_specs=VM,
        compiler_params=grant(20),
        cost_estimate=cost(2 * 512 * share * 256 * 384, 2 * jacobian.size),
        name="terms",
    )(turned, arrived)

    summed = summed_everywhere(tiles)

    chunks = 6
    flat_rows = ensemble.reshape(-1, members)
    updated = pl.pallas_call(
        solve_kernel,
        out_shape=jax.ShapeDtypeStruct(flat_rows.shape, BF16),
        in_specs=[VM, VM, ANY],
        out_specs=ANY,
        scratch_shapes=[
            pltpu.VMEM((members, members), F32),
            pltpu.VMEM((members, members), F32),
            pltpu.VMEM((members, 2 * members), F32),
            pltpu.VMEM(flat_rows.shape, BF16),
            pltpu.VMEM((chunks, flat_rows.shape[0] // chunks, members), BF16),
            pltpu.SemaphoreType.DMA,
            pltpu.SemaphoreType.DMA((chunks,)),
        ],
        compiler_params=grant(53),
        name="solve",
    )(summed, ensemble_vectors, flat_rows)
    return updated.reshape(ensemble.shape)


def solution(mesh):
    finer = Mesh(mesh.devices.reshape(8, 4, 8, 2), ("y", "x", "z", "c"))
    return jax.shard_map(
        local,
        mesh=finer,
        in_specs=(
            P(TILE, CHAN, None),
            P(TILE, CHAN, None),
            P(TILE, CHAN),
            P(),
            P(),
            P(),
            P(TILE, None, None),
            P(TILE),
            P(TILE),
        ),
        out_specs=P(TILE, CHAN, None),
        check_vma=False,
    )
```
